32 devices in a mesh: grp: 2 (over x), orbit: 4 (over y, core), chan: 4 (over z).
Axes of the slice: x: 2, y: 2, z: 4, core: 2. Of those that a mesh axis runs over, the one named last changes fastest.
Arguments:
- innovation: bfloat16 [65536, 1024], P(('grp', 'orbit'), 'chan'), parts along dimension 0, may hold values from -6 to 6
- perturbation: bfloat16 [65536, 1024], P(('grp', 'orbit'), 'chan'), parts along dimension 0, may hold values from -6 to 6
- quality: int32 [65536], P(('grp', 'orbit')), parts along dimension 0, may hold values 0 or 1
- neighbours: int32 [512, 6], P(('grp', 'orbit')), parts along dimension 0, may hold values from 0 to 255, as said below
- counts: int32 [512], P(('grp', 'orbit')), parts along dimension 0, may hold values from 1 to 6
- spatial_blocks: bfloat16 [512, 6, 128, 128], P(('grp', 'orbit')), parts along dimension 0, may hold values from -0.21875 to 0.21875
- chan_op: bfloat16 [1024, 1024], replicated, may hold values from -0.1875 to 0.1875
Outputs:
- weighted_innovation: bfloat16 [65536, 1024], P(('grp', 'orbit'), 'chan'), parts along dimension 0
- weighted_perturbation: bfloat16 [65536, 1024], P(('grp', 'orbit'), 'chan'), parts along dimension 0
The draws below stay inside these ranges and needn't reach their ends.
There are 2 independent parts, one for each index of `grp`. The reference program is written for one: setup_inputs(seed, part) draws one part's arguments, and reference() takes and returns one part's arrays. A program takes and returns all parts, laid end to end along the dimension named above; an argument that names none is the same for every part. Nothing has to cross between parts.
Inputs may be any that keep to these rules, and one draw needn't show every extreme that they name: `neighbours`: each neighbour of block b lies within 64 blocks of b.
All inputs are finite; a program needn't handle non-finite values. No bound on the sum of `quality` on one device may be relied on, other than what follows from the above.
Results may differ from the reference program's by a relative error of at most 0.0049.
Values may be sent and summed in bfloat16 or wider, within the bound.
No kernel may reach another device: no remote copies, remote signals or barrier semaphores. Data moves between devices by JAX's collectives and lax.ppermute only.
A program may use at most 256 MiB of HBM per device.

```python
import jax
import jax.numpy as jnp
from jax import lax

CH = 1024
BS = 128
NBR = 6
BLK_DEV = 64
REACH = 64
BLOCKS = 256
FOOT = 32768


def draw_neighbours(key, part):
    key = jax.random.fold_in(key, 11)
    blocks = jnp.arange(BLOCKS, dtype=jnp.int32)[:, None]
    offsets = jax.random.randint(key, (BLOCKS, NBR), -REACH, REACH + 1, dtype=jnp.int32)
    return jnp.clip(blocks + offsets, 0, BLOCKS - 1).astype(jnp.int32)


def draw_counts(key, part):
    key = jax.random.fold_in(key, 12)
    blocks = jnp.arange(BLOCKS, dtype=jnp.int32)
    owner = blocks // BLK_DEV
    ceiling = 1 + owner * 5 % NBR
    raw = jax.random.randint(key, (BLOCKS,), 0, 720720, dtype=jnp.int32)
    drawn = raw % ceiling + 1
    return jnp.where(blocks % BLK_DEV == 0, ceiling, drawn).astype(jnp.int32)


def with_ends(values, stream_key, smallest, largest):
    longest = values.shape.index(max(values.shape))
    spots = []
    for shift in (0, 1):
        where = [jax.random.randint(jax.random.fold_in(stream_key, axis), (), 0, length) for axis, length in enumerate(values.shape)]
        where[longest] = (where[longest] + shift) % values.shape[longest]
        spots.append(tuple(where))
    return values.at[spots[0]].set(smallest).at[spots[1]].set(largest)


def block_scale(own_key, dims, shards, least, high):
    factor_of = 1.0
    for axis_at, blocks in shards:
        steps = jax.random.uniform(jax.random.fold_in(jax.random.fold_in(own_key, 6), axis_at), (blocks,), jnp.float32, least / len(shards), high / len(shards))
        factor_of = factor_of * jnp.repeat(jnp.exp(steps), dims[axis_at] // blocks).reshape((-1,) + (1,) * (len(dims) - 1 - axis_at))
    return factor_of


def centred(key, shape, deviation, limit, split=(), held_as=jnp.bfloat16):
    array = jax.random.normal(key, shape, jnp.float32) * deviation
    if len(split) > 0:
        array = block_scale(key, shape, split, -0.22, 0.18) * array
    return jnp.clip(array, min=-limit, max=limit).astype(held_as)


def setup_inputs(seed: int = 0, part: int = 0) -> dict:
    keys = jax.random.split(jax.random.key(seed), 8)
    own_keys = jax.random.split(jax.random.fold_in(keys[7], part), 8)
    innovation = centred(own_keys[0], (FOOT, CH), 1.0, 6.0, ((0, 4), (1, 4)))
    perturbation = centred(own_keys[1], (FOOT, CH), 1.0, 6.0, ((0, 4), (1, 4)))
    quality = with_ends((jax.random.randint(own_keys[2], (FOOT,), 0, 8) < 7).astype(jnp.int32), jax.random.fold_in(own_keys[2], 1), 0, 1)
    neighbours = draw_neighbours(jax.random.fold_in(jax.random.fold_in(keys[7], part), 71), part)
    counts = draw_counts(jax.random.fold_in(jax.random.fold_in(keys[7], part), 71), part)
    spatial_blocks = centred(own_keys[5], (BLOCKS, NBR, BS, BS), (NBR * BS) ** -0.5, 0.21875, ((0, 4),))
    chan_op = centred(keys[6], (CH, CH), CH ** -0.5, 0.1875)
    return dict(innovation=innovation, perturbation=perturbation, quality=quality, neighbours=neighbours, counts=counts, spatial_blocks=spatial_blocks, chan_op=chan_op)


def reference(innovation, perturbation, quality, neighbours, counts, spatial_blocks, chan_op):
    keep = quality.astype(jnp.bfloat16)[:, None]
    live = (jnp.arange(NBR, dtype=jnp.int32)[None, :] < counts[:, None]).astype(jnp.bfloat16)
    weights = spatial_blocks * live[:, :, None, None]

    def weigh(vector):
        tiles = (vector * keep).reshape(BLOCKS, BS, CH)

        def per_block(pair):
            block_w, block_ids = pair
            picked = tiles[block_ids.astype(jnp.int32)]
            return jnp.einsum("sij,sjc->ic", block_w.astype(jnp.float32), picked.astype(jnp.float32)).astype(jnp.bfloat16)

        spatial = lax.map(per_block, (weights, neighbours)).reshape(FOOT, CH)
        mixed = jnp.dot(spatial, chan_op, preferred_element_type=jnp.float32)
        return (mixed * keep.astype(jnp.float32)).astype(jnp.bfloat16)

    return weigh(innovation), weigh(perturbation)
```

```python
import functools

import jax
import jax.numpy as jnp
from jax import lax
from jax.experimental import pallas as pl
from jax.experimental.pallas import tpu as pltpu
from jax.sharding import PartitionSpec as P

VMEM_LIMIT = 48 * 1024 * 1024
ALIGN = 16
GROUP = 8


def params():
    return pltpu.CompilerParams(
        dimension_semantics=("arbitrary",), vmem_limit_bytes=VMEM_LIMIT
    )


def plan_kernel(quality_ref, pos_ref, offs_ref):
    blocks, rows = quality_ref.shape
    keep = quality_ref[...]
    ones = keep.astype(jnp.float32).astype(jnp.bfloat16)

    def tri(size, strict):
        a = lax.broadcasted_iota(jnp.int32, (size, size), 0)
        b = lax.broadcasted_iota(jnp.int32, (size, size), 1)
        return jnp.where(a < b if strict else a <= b, 1.0, 0.0).astype(jnp.bfloat16)

    within = jnp.dot(ones, tri(rows, True), preferred_element_type=jnp.float32)
    total = jnp.sum(keep.astype(jnp.float32), axis=1, keepdims=True)
    wide = jnp.broadcast_to(total, (blocks, rows)).astype(jnp.bfloat16)
    a = lax.broadcasted_iota(jnp.int32, (blocks, blocks), 0)
    b = lax.broadcasted_iota(jnp.int32, (blocks, blocks), 1)
    below = jnp.where(b < a, 1.0, 0.0).astype(jnp.bfloat16)
    before = jnp.dot(below, wide, preferred_element_type=jnp.float32)
    pos = (before + within).astype(jnp.int32)
    pos_ref[...] = jnp.where(keep > 0, pos, -1)
    offs_ref[...] = before.astype(jnp.int32)


def plan(quality, block_rows):
    nblk = quality.shape[0] // block_rows
    shape = jax.ShapeDtypeStruct((nblk, block_rows), jnp.int32)
    pos, offs = pl.pallas_call(plan_kernel, out_shape=(shape, shape))(
        quality.reshape(nblk, block_rows)
    )
    return pos, offs[:, 0]


def window(offs_ref, block):
    return pl.multiple_of((offs_ref[block] // ALIGN) * ALIGN, ALIGN)


def one_hot(pos, start, block_rows):
    span = block_rows + ALIGN
    at = lax.broadcasted_iota(jnp.int32, (span, block_rows), 0) + start
    return jnp.where(at == pos, 1.0, 0.0).astype(jnp.bfloat16)


def put_compact(packed, pos, start, tile):
    block_rows = tile.shape[0]
    part = jnp.dot(
        one_hot(pos, start, block_rows), tile, preferred_element_type=jnp.float32
    ).astype(jnp.bfloat16)
    packed[pl.ds(start, ALIGN), :] = packed[pl.ds(start, ALIGN), :] + part[:ALIGN]
    packed[pl.ds(pl.multiple_of(start + ALIGN, ALIGN), block_rows), :] = part[ALIGN:]


def clear(ref):
    rows = ref.shape[0]
    step = ALIGN

    def body(i, carry):
        ref[pl.ds(pl.multiple_of(i * step, step), step), :] = jnp.zeros(
            (step, ref.shape[1]), ref.dtype
        )
        return carry

    lax.fori_loop(0, rows // step, body, 0, unroll=8 if rows // step % 8 == 0 else 1)


def part_copies(packed, outs, sems, me, sizes, count, outward):
    copies = []
    base = 0
    at = 0
    for size in sizes:
        for shift in range(count):
            owner = lax.rem(me + (shift if outward else count - shift), count)
            where = packed.at[pl.ds(pl.multiple_of(base + owner * size, ALIGN), size), :]
            if outward:
                copies.append(pltpu.make_async_copy(where, outs[at], sems.at[at]))
            else:
                copies.append(pltpu.make_async_copy(outs[at], where, sems.at[at]))
            at += 1
        base += size * count
    return copies


def compact_kernel(sizes, count, me_ref, offs_ref, pos_ref, v_ref, *rest):
    outs, (packed, sems) = rest[:-2], rest[-2:]
    block_rows = pos_ref.shape[1]
    step = pl.program_id(0)

    @pl.when(step == 0)
    def _():
        clear(packed)

    for i in range(GROUP):
        put_compact(
            packed,
            pos_ref[i : i + 1, :],
            window(offs_ref, step * GROUP + i),
            v_ref[i * block_rows : (i + 1) * block_rows, :],
        )

    @pl.when(step == pl.num_programs(0) - 1)
    def _():
        copies = part_copies(packed, outs, sems, me_ref[0], sizes, count, True)
        for copy in copies:
            copy.start()
        for copy in copies:
            copy.wait()


def part_shapes(sizes, count, width):
    return tuple(
        jax.ShapeDtypeStruct((size, width), jnp.bfloat16) for size in sizes for _ in range(count)
    )


def compact(v, pos, offs, me, sizes, count):
    rows, width = v.shape
    nblk, block_rows = pos.shape
    shapes = part_shapes(sizes, count, width)
    return pl.pallas_call(
        functools.partial(compact_kernel, sizes, count),
        out_shape=shapes,
        grid_spec=pltpu.PrefetchScalarGridSpec(
            num_scalar_prefetch=2,
            grid=(nblk // GROUP,),
            in_specs=[
                pl.BlockSpec((GROUP, block_rows), lambda i, *_: (i, 0)),
                pl.BlockSpec((GROUP * block_rows, width), lambda i, *_: (i, 0)),
            ],
            out_specs=[pl.BlockSpec(memory_space=pl.ANY)] * len(shapes),
            scratch_shapes=[
                pltpu.VMEM((rows + ALIGN, width), jnp.bfloat16),
                pltpu.SemaphoreType.DMA((len(shapes),)),
            ],
        ),
        compiler_params=params(),
        cost_estimate=pl.CostEstimate(
            flops=2 * rows * 144 * width, bytes_accessed=4 * rows * width, transcendentals=0
        ),
    )(me, offs, pos, v)


def expand_kernel(sizes, count, me_ref, offs_ref, pos_ref, *rest):
    ins, (out_ref, packed, sems) = rest[:-3], rest[-3:]
    block_rows = pos_ref.shape[1]
    span = block_rows + ALIGN
    rows = packed.shape[0] - ALIGN
    step = pl.program_id(0)

    @pl.when(step == 0)
    def _():
        copies = part_copies(packed, ins, sems, me_ref[0], sizes, count, False)
        for copy in copies:
            copy.start()
        packed[rows:, :] = jnp.zeros((ALIGN, packed.shape[1]), packed.dtype)
        for copy in copies:
            copy.wait()

    for i in range(GROUP):
        start = window(offs_ref, step * GROUP + i)
        out_ref[i * block_rows : (i + 1) * block_rows, :] = lax.dot_general(
            one_hot(pos_ref[i : i + 1, :], start, block_rows),
            packed[pl.ds(start, span), :],
            (((0,), (0,)), ((), ())),
            preferred_element_type=jnp.float32,
        ).astype(jnp.bfloat16)


def expand(parts, pos, offs, me, sizes, count):
    nblk, block_rows = pos.shape
    rows = nblk * block_rows
    width = parts[0].shape[1]
    return pl.pallas_call(
        functools.partial(expand_kernel, sizes, count),
        out_shape=jax.ShapeDtypeStruct((rows, width), jnp.bfloat16),
        grid_spec=pltpu.PrefetchScalarGridSpec(
            num_scalar_prefetch=2,
            grid=(nblk // GROUP,),
            in_specs=[pl.BlockSpec((GROUP, block_rows), lambda i, *_: (i, 0))]
            + [pl.BlockSpec(memory_space=pl.ANY)] * len(parts),
            out_specs=pl.BlockSpec((GROUP * block_rows, width), lambda i, *_: (i, 0)),
            scratch_shapes=[
                pltpu.VMEM((rows + ALIGN, width), jnp.bfloat16),
                pltpu.SemaphoreType.DMA((len(parts),)),
            ],
        ),
        compiler_params=params(),
        cost_estimate=pl.CostEstimate(
            flops=2 * rows * 144 * width, bytes_accessed=4 * rows * width, transcendentals=0
        ),
    )(me, offs, pos, *parts)


def spatial_kernel(
    sizes, count, slots, me_ref, offs_ref, ids_ref, counts_ref, pos_ref, keep_ref, weight_ref,
    left, own, right, *rest
):
    block_rows = pos_ref.shape[1]
    step = pl.program_id(0)
    last = pl.num_programs(0) - 1
    if sizes is None:
        out_ref, tiles, halo_sems = rest
    else:
        outs, (tiles, halo_sems, packed, sems) = rest[:-4], rest[-4:]
    rows = tiles.shape[0] // 3

    @pl.when(step == 0)
    def _():
        copies = [
            pltpu.make_async_copy(source, tiles.at[pl.ds(i * rows, rows), :], halo_sems.at[i])
            for i, source in enumerate((left, own, right))
        ]
        for copy in copies:
            copy.start()
        if sizes is not None:
            clear(packed)
        for copy in copies:
            copy.wait()

    for i in range(GROUP):
        block = step * GROUP + i
        used = counts_ref[block]
        weights = []
        picked = []
        for slot in range(slots):
            at = ids_ref[block * slots + slot]
            live = jnp.where(slot < used, 1.0, 0.0)
            scale = jnp.broadcast_to(live, (1, block_rows))
            if sizes is not None:
                scale = scale * keep_ref[pl.ds(at, 1), :]
            weights.append(weight_ref[i, slot] * scale.astype(jnp.bfloat16))
            start = pl.multiple_of(at * block_rows, block_rows)
            picked.append(tiles[pl.ds(start, block_rows), :])
        spatial = jnp.dot(
            jnp.concatenate(weights, axis=1),
            jnp.concatenate(picked, axis=0),
            preferred_element_type=jnp.float32,
        ).astype(jnp.bfloat16)
        pos = pos_ref[i : i + 1, :]
        if sizes is None:
            a = lax.broadcasted_iota(jnp.int32, (block_rows, block_rows), 0)
            b = lax.broadcasted_iota(jnp.int32, (block_rows, block_rows), 1)
            kept = jnp.where((a == b) & (pos >= 0), 1.0, 0.0).astype(jnp.bfloat16)
            out_ref[i * block_rows : (i + 1) * block_rows, :] = jnp.dot(
                kept, spatial, preferred_element_type=jnp.float32
            ).astype(jnp.bfloat16)
        else:
            put_compact(packed, pos, window(offs_ref, block), spatial)

    if sizes is not None:

        @pl.when(step == last)
        def _():
            copies = part_copies(packed, outs, sems, me_ref[0], sizes, count, True)
            for copy in copies:
                copy.start()
            for copy in copies:
                copy.wait()


def spatial(halo, weights, keep, ids, counts, pos, offs, me, sizes, count):
    rows, width = halo[1].shape
    nblk, block_rows = pos.shape
    slots = weights.shape[1]
    any_spec = pl.BlockSpec(memory_space=pl.ANY)
    scratch = [
        pltpu.VMEM((3 * rows, width), jnp.bfloat16),
        pltpu.SemaphoreType.DMA((3,)),
    ]
    if sizes is None:
        shapes = jax.ShapeDtypeStruct((rows, width), jnp.bfloat16)
        out_specs = pl.BlockSpec((GROUP * block_rows, width), lambda i, *_: (i, 0))
    else:
        shapes = part_shapes(sizes, count, width)
        out_specs = [any_spec] * len(shapes)
        scratch += [
            pltpu.VMEM((rows + ALIGN, width), jnp.bfloat16),
            pltpu.SemaphoreType.DMA((len(shapes),)),
        ]
    return pl.pallas_call(
        functools.partial(spatial_kernel, sizes, count, slots),
        out_shape=shapes,
        grid_spec=pltpu.PrefetchScalarGridSpec(
            num_scalar_prefetch=4,
            grid=(nblk // GROUP,),
            in_specs=[
                pl.BlockSpec((GROUP, block_rows), lambda i, *_: (i, 0)),
                pl.BlockSpec(keep.shape, lambda i, *_: (0, 0)),
                pl.BlockSpec((GROUP, slots, block_rows, block_rows), lambda i, *_: (i, 0, 0, 0)),
                any_spec,
                any_spec,
                any_spec,
            ],
            out_specs=out_specs,
            scratch_shapes=scratch,
        ),
        compiler_params=params(),
        cost_estimate=pl.CostEstimate(
            flops=2 * rows * slots * block_rows * width,
            bytes_accessed=8 * rows * width + 2 * rows * slots * block_rows,
            transcendentals=0,
        ),
    )(me, offs, ids, counts, pos, keep, weights, *halo)


def mix_kernel(count, me_ref, op_ref, *rest):
    ins, outs, (rolled, sems) = rest[:count], rest[count : 2 * count], rest[2 * count :]
    width = ins[0].shape[1]
    me = me_ref[0]

    @pl.when(pl.program_id(0) == 0)
    def _():
        copies = []
        for shift in range(count):
            source = lax.rem(me + count - shift, count)
            copies.append(
                pltpu.make_async_copy(
                    op_ref.at[pl.ds(pl.multiple_of(source * width, ALIGN), width), :],
                    rolled.at[pl.ds(shift * width, width), :],
                    sems.at[shift],
                )
            )
        for copy in copies:
            copy.start()
        for copy in copies:
            copy.wait()

    row = jnp.concatenate([part[...] for part in ins], axis=1)
    for shift in range(count):
        dest = lax.rem(me + shift, count)
        columns = rolled[:, pl.ds(pl.multiple_of(dest * width, 128), width)]
        outs[shift][...] = jnp.dot(row, columns, preferred_element_type=jnp.float32).astype(
            jnp.bfloat16
        )


def mix(parts, chan_op, me):
    count = len(parts)
    rows, width = parts[0].shape
    tiles = [t for t in range(ALIGN, min(rows, 640) + 1, ALIGN) if rows % t == 0]
    tile = tiles[-1]
    spec = pl.BlockSpec((tile, width), lambda i, *_: (i, 0))
    return pl.pallas_call(
        functools.partial(mix_kernel, count),
        out_shape=part_shapes((rows,), count, width),
        grid_spec=pltpu.PrefetchScalarGridSpec(
            num_scalar_prefetch=1,
            grid=(rows // tile,),
            in_specs=[pl.BlockSpec(memory_space=pl.ANY)] + [spec] * count,
            out_specs=[spec] * count,
            scratch_shapes=[
                pltpu.VMEM(chan_op.shape, jnp.bfloat16),
                pltpu.SemaphoreType.DMA((count,)),
            ],
        ),
        compiler_params=params(),
        cost_estimate=pl.CostEstimate(
            flops=2 * rows * chan_op.shape[0] * chan_op.shape[1],
            bytes_accessed=4 * rows * width * count + 2 * chan_op.size,
            transcendentals=0,
        ),
    )(me, chan_op, *parts)


def exchange(parts):
    count = len(parts)
    return (parts[0],) + tuple(
        lax.ppermute(parts[k], "chan", [(i, (i + k) % count) for i in range(count)])
        for k in range(1, count)
    )


def neighbours_of(x):
    count = lax.axis_size("orbit")
    up = [(i, i + 1) for i in range(count - 1)]
    down = [(i + 1, i) for i in range(count - 1)]
    return lax.ppermute(x, "orbit", up), x, lax.ppermute(x, "orbit", down)


def shards(innovation, perturbation, quality, neighbours, counts, spatial_blocks, chan_op):
    rows, width = innovation.shape
    block_rows = spatial_blocks.shape[2]
    nblk = rows // block_rows
    count = lax.axis_size("chan")
    unit = ALIGN * count
    main = -(-rows * 57 // (64 * unit)) * unit
    sizes = (main // count, (rows - main) // count)

    me = lax.axis_index("chan").astype(jnp.int32).reshape(1)
    first = (lax.axis_index("orbit") - 1) * nblk
    ids = jnp.clip(neighbours - first, 0, 3 * nblk - 1).reshape(-1)
    more = jnp.sum(quality, dtype=jnp.int32) > main
    more = lax.pmax(more.astype(jnp.int32), ("grp", "orbit"))

    halo_p = neighbours_of(perturbation)
    keep = quality.reshape(nblk, block_rows).astype(jnp.float32)
    keep = jnp.concatenate(neighbours_of(keep), axis=0)
    pos, offs = plan(quality, block_rows)

    parts_i = compact(innovation, pos, offs, me, sizes, count)
    there_i = exchange(parts_i[:count])
    parts_p = spatial(
        halo_p, spatial_blocks, keep, ids, counts, pos, offs, me, sizes, count
    )
    there_p = exchange(parts_p[:count])

    def rest(parts):
        return tuple(exchange(mix(exchange(p), chan_op, me)) for p in parts)

    def nothing(parts):
        return jax.tree.map(jnp.zeros_like, parts)

    rest_i, rest_p = lax.cond(more > 0, rest, nothing, (parts_i[count:], parts_p[count:]))

    back_i = exchange(mix(there_i, chan_op, me))
    mixed_i = expand(back_i + rest_i, pos, offs, me, sizes, count)
    halo_i = neighbours_of(mixed_i)
    back_p = exchange(mix(there_p, chan_op, me))
    out_i = spatial(halo_i, spatial_blocks, keep, ids, counts, pos, offs, me, None, count)
    out_p = expand(back_p + rest_p, pos, offs, me, sizes, count)
    return out_i, out_p


def solution(mesh):
    placed = (
        P(("grp", "orbit"), "chan"),
        P(("grp", "orbit"), "chan"),
        P(("grp", "orbit")),
        P(("grp", "orbit"), None),
        P(("grp", "orbit")),
        P(("grp", "orbit"), None, None, None),
        P(),
    )
    return jax.shard_map(
        shards,
        mesh=mesh,
        in_specs=placed,
        out_specs=(P(("grp", "orbit"), "chan"), P(("grp", "orbit"), "chan")),
        check_vma=False,
    )
```

```python
import functools

import jax
import jax.numpy as jnp
from jax import lax
from jax.experimental import pallas as pl
from jax.experimental.pallas import tpu as pltpu
from jax.sharding import PartitionSpec as P

VMEM_LIMIT = 48 * 1024 * 1024
ALIGN = 16
DEPTH = 3
GROUP = 8


def params():
    return pltpu.CompilerParams(
        dimension_semantics=("arbitrary",), vmem_limit_bytes=VMEM_LIMIT
    )


def plan_kernel(quality_ref, pos_ref, offs_ref):
    blocks, rows = quality_ref.shape
    keep = quality_ref[...]
    ones = keep.astype(jnp.float32).astype(jnp.bfloat16)

    def tri(size, strict):
        a = lax.broadcasted_iota(jnp.int32, (size, size), 0)
        b = lax.broadcasted_iota(jnp.int32, (size, size), 1)
        return jnp.where(a < b if strict else a <= b, 1.0, 0.0).astype(jnp.bfloat16)

    within = jnp.dot(ones, tri(rows, True), preferred_element_type=jnp.float32)
    total = jnp.sum(keep.astype(jnp.float32), axis=1, keepdims=True)
    wide = jnp.broadcast_to(total, (blocks, rows)).astype(jnp.bfloat16)
    a = lax.broadcasted_iota(jnp.int32, (blocks, blocks), 0)
    b = lax.broadcasted_iota(jnp.int32, (blocks, blocks), 1)
    below = jnp.where(b < a, 1.0, 0.0).astype(jnp.bfloat16)
    before = jnp.dot(below, wide, preferred_element_type=jnp.float32)
    pos = (before + within).astype(jnp.int32)
    pos_ref[...] = jnp.where(keep > 0, pos, -1)
    offs_ref[...] = before.astype(jnp.int32)


def plan(quality, block_rows):
    nblk = quality.shape[0] // block_rows
    shape = jax.ShapeDtypeStruct((nblk, block_rows), jnp.int32)
    pos, offs = pl.pallas_call(plan_kernel, out_shape=(shape, shape))(
        quality.reshape(nblk, block_rows)
    )
    return pos, offs[:, 0]


def window(offs_ref, block):
    return pl.multiple_of((offs_ref[block] // ALIGN) * ALIGN, ALIGN)


def one_hot(pos, start, block_rows):
    span = block_rows + ALIGN
    at = lax.broadcasted_iota(jnp.int32, (span, block_rows), 0) + start
    return jnp.where(at == pos, 1.0, 0.0).astype(jnp.bfloat16)


def kept_rows(pos, start, tile):
    return jnp.dot(
        one_hot(pos, start, tile.shape[0]), tile, preferred_element_type=jnp.float32
    ).astype(jnp.bfloat16)


def put_rows(packed, start, part):
    rest = part.shape[0] - ALIGN
    packed[pl.ds(start, ALIGN), :] = packed[pl.ds(start, ALIGN), :] + part[:ALIGN]
    packed[pl.ds(pl.multiple_of(start + ALIGN, ALIGN), rest), :] = part[ALIGN:]


def clear(ref):
    rows = ref.shape[0]
    step = ALIGN

    def body(i, carry):
        ref[pl.ds(pl.multiple_of(i * step, step), step), :] = jnp.zeros(
            (step, ref.shape[1]), ref.dtype
        )
        return carry

    lax.fori_loop(0, rows // step, body, 0, unroll=8 if rows // step % 8 == 0 else 1)


def part_copies(packed, parts, sems, me, outward):
    count = len(parts)
    size = parts[0].shape[0]
    copies = []
    for shift, part in enumerate(parts):
        owner = lax.rem(me + (shift if outward else count - shift), count)
        where = packed.at[pl.ds(pl.multiple_of(owner * size, ALIGN), size), :]
        ends = (where, part) if outward else (part, where)
        copies.append(pltpu.make_async_copy(*ends, sems.at[shift]))
    return copies


def compact_kernel(me_ref, offs_ref, pos_ref, v_ref, *rest):
    outs, (packed, sems) = rest[:-2], rest[-2:]
    block_rows = pos_ref.shape[1]
    step = pl.program_id(0)

    @pl.when(step == 0)
    def _():
        clear(packed)

    starts = [window(offs_ref, step * GROUP + i) for i in range(GROUP)]
    found = [
        kept_rows(
            pos_ref[i : i + 1, :], starts[i], v_ref[i * block_rows : (i + 1) * block_rows, :]
        )
        for i in range(GROUP)
    ]
    for start, part in zip(starts, found):
        put_rows(packed, start, part)

    @pl.when(step == pl.num_programs(0) - 1)
    def _():
        copies = part_copies(packed, outs, sems, me_ref[0], True)
        for copy in copies:
            copy.start()
        for copy in copies:
            copy.wait()


def part_shapes(size, count, width):
    return (jax.ShapeDtypeStruct((size, width), jnp.bfloat16),) * count


def compact(v, pos, offs, me, size, count):
    rows, width = v.shape
    nblk, block_rows = pos.shape
    shapes = part_shapes(size, count, width)
    return pl.pallas_call(
        compact_kernel,
        out_shape=shapes,
        grid_spec=pltpu.PrefetchScalarGridSpec(
            num_scalar_prefetch=2,
            grid=(nblk // GROUP,),
            in_specs=[
                pl.BlockSpec((GROUP, block_rows), lambda i, *_: (i, 0)),
                pl.BlockSpec((GROUP * block_rows, width), lambda i, *_: (i, 0)),
            ],
            out_specs=[pl.BlockSpec(memory_space=pl.ANY)] * len(shapes),
            scratch_shapes=[
                pltpu.VMEM((rows + ALIGN, width), jnp.bfloat16),
                pltpu.SemaphoreType.DMA((len(shapes),)),
            ],
        ),
        compiler_params=params(),
        cost_estimate=pl.CostEstimate(flops=1, bytes_accessed=1, transcendentals=0),
    )(me, offs, pos, v)


def expand_kernel(me_ref, offs_ref, pos_ref, *rest):
    ins, (out_ref, packed, sems) = rest[:-3], rest[-3:]
    block_rows = pos_ref.shape[1]
    span = block_rows + ALIGN
    step = pl.program_id(0)

    @pl.when(step == 0)
    def _():
        copies = part_copies(packed, ins, sems, me_ref[0], False)
        for copy in copies:
            copy.start()
        clear(packed.at[pl.ds(len(ins) * ins[0].shape[0], packed.shape[0] - len(ins) * ins[0].shape[0]), :])
        for copy in copies:
            copy.wait()

    for i in range(GROUP):
        start = window(offs_ref, step * GROUP + i)
        out_ref[i * block_rows : (i + 1) * block_rows, :] = lax.dot_general(
            one_hot(pos_ref[i : i + 1, :], start, block_rows),
            packed[pl.ds(start, span), :],
            (((0,), (0,)), ((), ())),
            preferred_element_type=jnp.float32,
        ).astype(jnp.bfloat16)


def expand(parts, pos, offs, me):
    nblk, block_rows = pos.shape
    rows = nblk * block_rows
    width = parts[0].shape[1]
    return pl.pallas_call(
        expand_kernel,
        out_shape=jax.ShapeDtypeStruct((rows, width), jnp.bfloat16),
        grid_spec=pltpu.PrefetchScalarGridSpec(
            num_scalar_prefetch=2,
            grid=(nblk // GROUP,),
            in_specs=[pl.BlockSpec((GROUP, block_rows), lambda i, *_: (i, 0))]
            + [pl.BlockSpec(memory_space=pl.ANY)] * len(parts),
            out_specs=pl.BlockSpec((GROUP * block_rows, width), lambda i, *_: (i, 0)),
            scratch_shapes=[
                pltpu.VMEM((rows + ALIGN, width), jnp.bfloat16),
                pltpu.SemaphoreType.DMA((len(parts),)),
            ],
        ),
        compiler_params=params(),
        cost_estimate=pl.CostEstimate(flops=1, bytes_accessed=1, transcendentals=0),
    )(me, offs, pos, *parts)


def spatial_kernel(
    compacting, slots, me_ref, offs_ref, ids_ref, counts_ref, pos_ref, weight_ref,
    left, own, right, *rest
):
    block_rows = pos_ref.shape[1]
    step = pl.program_id(0)
    last = pl.num_programs(0) - 1
    if not compacting:
        out_ref, tiles, halo_sems = rest
    else:
        outs, (tiles, halo_sems, packed, sems) = rest[:-4], rest[-4:]
    rows = tiles.shape[0] // 3

    @pl.when(step == 0)
    def _():
        copies = [
            pltpu.make_async_copy(source, tiles.at[pl.ds(i * rows, rows), :], halo_sems.at[i])
            for i, source in enumerate((left, own, right))
        ]
        for copy in copies:
            copy.start()
        if compacting:
            clear(packed)
        for copy in copies:
            copy.wait()

    found = []
    for i in range(GROUP):
        block = step * GROUP + i
        used = counts_ref[block]
        weights = []
        picked = []
        for slot in range(slots):
            at = ids_ref[block * slots + slot]
            live = jnp.where(slot < used, 1.0, 0.0)
            weights.append(weight_ref[i, slot] * live.astype(jnp.bfloat16))
            start = pl.multiple_of(at * block_rows, block_rows)
            picked.append(tiles[pl.ds(start, block_rows), :])
        spatial = jnp.dot(
            jnp.concatenate(weights, axis=1),
            jnp.concatenate(picked, axis=0),
            preferred_element_type=jnp.float32,
        ).astype(jnp.bfloat16)
        pos = pos_ref[i : i + 1, :]
        if not compacting:
            a = lax.broadcasted_iota(jnp.int32, (block_rows, block_rows), 0)
            b = lax.broadcasted_iota(jnp.int32, (block_rows, block_rows), 1)
            kept = jnp.where((a == b) & (pos >= 0), 1.0, 0.0).astype(jnp.bfloat16)
            out_ref[i * block_rows : (i + 1) * block_rows, :] = jnp.dot(
                kept, spatial, preferred_element_type=jnp.float32
            ).astype(jnp.bfloat16)
        else:
            start = window(offs_ref, block)
            found.append((start, kept_rows(pos, start, spatial)))

    for start, part in found:
        put_rows(packed, start, part)

    if compacting:

        @pl.when(step == last)
        def _():
            copies = part_copies(packed, outs, sems, me_ref[0], True)
            for copy in copies:
                copy.start()
            for copy in copies:
                copy.wait()


def spatial(halo, weights, ids, counts, pos, offs, me, size, count):
    rows, width = halo[1].shape
    nblk, block_rows = pos.shape
    slots = weights.shape[1]
    any_spec = pl.BlockSpec(memory_space=pl.ANY)
    scratch = [
        pltpu.VMEM((3 * rows, width), jnp.bfloat16),
        pltpu.SemaphoreType.DMA((3,)),
    ]
    if size is None:
        shapes = jax.ShapeDtypeStruct((rows, width), jnp.bfloat16)
        out_specs = pl.BlockSpec((GROUP * block_rows, width), lambda i, *_: (i, 0))
    else:
        shapes = part_shapes(size, count, width)
        out_specs = [any_spec] * len(shapes)
        scratch += [
            pltpu.VMEM((rows + ALIGN, width), jnp.bfloat16),
            pltpu.SemaphoreType.DMA((len(shapes),)),
        ]
    return pl.pallas_call(
        functools.partial(spatial_kernel, size is not None, slots),
        out_shape=shapes,
        grid_spec=pltpu.PrefetchScalarGridSpec(
            num_scalar_prefetch=4,
            grid=(nblk // GROUP,),
            in_specs=[
                pl.BlockSpec((GROUP, block_rows), lambda i, *_: (i, 0)),
                pl.BlockSpec((GROUP, slots, block_rows, block_rows), lambda i, *_: (i, 0, 0, 0)),
                any_spec,
                any_spec,
                any_spec,
            ],
            out_specs=out_specs,
            scratch_shapes=scratch,
        ),
        compiler_params=params(),
        cost_estimate=pl.CostEstimate(flops=1, bytes_accessed=1, transcendentals=0),
    )(me, offs, ids, counts, pos, weights, *halo)


def mix_kernel(count, me_ref, op_ref, *rest):
    ins, outs, (rolled, sems) = rest[:count], rest[count : 2 * count], rest[2 * count :]
    width = ins[0].shape[1]
    me = me_ref[0]

    @pl.when(pl.program_id(0) == 0)
    def _():
        copies = []
        for shift in range(count):
            source = lax.rem(me + count - shift, count)
            copies.append(
                pltpu.make_async_copy(
                    op_ref.at[pl.ds(pl.multiple_of(source * width, ALIGN), width), :],
                    rolled.at[pl.ds(shift * width, width), :],
                    sems.at[shift],
                )
            )
        for copy in copies:
            copy.start()
        for copy in copies:
            copy.wait()

    row = jnp.concatenate([part[...] for part in ins], axis=1)
    for shift in range(count):
        dest = lax.rem(me + shift, count)
        columns = rolled[:, pl.ds(pl.multiple_of(dest * width, 128), width)]
        outs[shift][...] = jnp.dot(row, columns, preferred_element_type=jnp.float32).astype(
            jnp.bfloat16
        )


def mix(parts, chan_op, me):
    count = len(parts)
    rows, width = parts[0].shape
    tiles = [t for t in range(ALIGN, min(rows, 640) + 1, ALIGN) if rows % t == 0]
    tile = tiles[-1]
    spec = pl.BlockSpec((tile, width), lambda i, *_: (i, 0))
    return pl.pallas_call(
        functools.partial(mix_kernel, count),
        out_shape=part_shapes(rows, count, width),
        grid_spec=pltpu.PrefetchScalarGridSpec(
            num_scalar_prefetch=1,
            grid=(rows // tile,),
            in_specs=[pl.BlockSpec(memory_space=pl.ANY)] + [spec] * count,
            out_specs=[spec] * count,
            scratch_shapes=[
                pltpu.VMEM(chan_op.shape, jnp.bfloat16),
                pltpu.SemaphoreType.DMA((count,)),
            ],
        ),
        compiler_params=params(),
        cost_estimate=pl.CostEstimate(flops=1, bytes_accessed=1, transcendentals=0),
    )(me, chan_op, *parts)


class Line:
    def __init__(self, depth):
        self.depth = depth
        self.done = []

    def exchange(self, parts):
        count = len(parts)
        arrived = list(parts)
        for shift in sorted(range(1, count), key=lambda k: min(k, count - k)):
            part = parts[shift]
            if len(self.done) >= self.depth:
                part = after(part, self.done[-self.depth])
            arrived[shift] = lax.ppermute(
                part, "chan", [(i, (i + shift) % count) for i in range(count)]
            )
            self.done.append(arrived[shift])
        return tuple(arrived)


def after(values, *others):
    return lax.optimization_barrier((values, others))[0]


def neighbours_of(x):
    count = lax.axis_size("orbit")
    up = [(i, i + 1) for i in range(count - 1)]
    down = [(i + 1, i) for i in range(count - 1)]
    return lax.ppermute(x, "orbit", up), x, lax.ppermute(x, "orbit", down)


def weigh(
    innovation, perturbation, quality, neighbours, counts, spatial_blocks, chan_op, capacity, watch
):
    rows, width = innovation.shape
    block_rows = spatial_blocks.shape[2]
    nblk = rows // block_rows
    count = lax.axis_size("chan")
    size = capacity // count

    me = lax.axis_index("chan").astype(jnp.int32).reshape(1)
    first = (lax.axis_index("orbit") - 1) * nblk
    ids = jnp.clip(neighbours - first, 0, 3 * nblk - 1).reshape(-1)
    pos, offs = plan(quality, block_rows)

    def spread(halo, room):
        return spatial(halo, spatial_blocks, ids, counts, pos, offs, me, room, count)

    parts_i = compact(innovation, pos, offs, me, size, count)
    line = Line(DEPTH)
    there_i = line.exchange(parts_i)
    perturbation, quality = after((perturbation, quality), parts_i[0])
    masked_p = perturbation * quality.astype(jnp.bfloat16)[:, None]
    parts_p = spread(neighbours_of(masked_p), size)
    there_p = line.exchange(parts_p)

    mixed_i = mix(after(there_i, parts_p[0]), chan_op, me)
    back_i = line.exchange(mixed_i)
    mixed_p = mix(after(there_p, mixed_i[0]), chan_op, me)
    back_p = line.exchange(mixed_p)
    seen = watch(after(quality, mixed_p[0]))

    wide_i = expand(after(back_i, mixed_p[0]), pos, offs, me)
    out_i = spread(neighbours_of(wide_i), None)
    out_p = expand(after(back_p, out_i), pos, offs, me)
    return (out_i, out_p), seen


def shards(innovation, perturbation, quality, *others):
    rows = innovation.shape[0]
    unit = ALIGN * lax.axis_size("chan")
    capacity = -(-rows * 57 // (64 * unit)) * unit
    given = (innovation, perturbation, quality, *others)

    def overfull(quality):
        more = jnp.sum(quality, dtype=jnp.int32) > capacity
        return lax.pmax(more.astype(jnp.int32), ("grp", "orbit"))

    packed, more = weigh(*given, capacity, overfull)
    return lax.cond(
        more > 0,
        lambda given, packed: weigh(*given, rows, lambda quality: None)[0],
        lambda given, packed: packed,
        given,
        packed,
    )


def solution(mesh):
    placed = (
        P(("grp", "orbit"), "chan"),
        P(("grp", "orbit"), "chan"),
        P(("grp", "orbit")),
        P(("grp", "orbit"), None),
        P(("grp", "orbit")),
        P(("grp", "orbit"), None, None, None),
        P(),
    )
    return jax.shard_map(
        shards,
        mesh=mesh,
        in_specs=placed,
        out_specs=(P(("grp", "orbit"), "chan"), P(("grp", "orbit"), "chan")),
        check_vma=False,
    )
```

```python
import functools

import jax
import jax.numpy as jnp
from jax import lax
from jax.experimental import pallas as pl
from jax.experimental.pallas import tpu as pltpu
from jax.sharding import PartitionSpec as P

VMEM_LIMIT = 48 * 1024 * 1024
ALIGN = 16
DEPTH = 3
PAIR = 2
EXPAND = 1
GROUP = 8


def params():
    return pltpu.CompilerParams(
        dimension_semantics=("arbitrary",), vmem_limit_bytes=VMEM_LIMIT
    )


def plan(quality, pos_ref, offs_ref):
    blocks, rows = quality.shape
    ones = quality.astype(jnp.float32).astype(jnp.bfloat16)

    def ahead(size):
        a = lax.broadcasted_iota(jnp.int32, (size, size), 0)
        b = lax.broadcasted_iota(jnp.int32, (size, size), 1)
        return jnp.where(a < b, 1.0, 0.0).astype(jnp.bfloat16)

    def dot(a, b, dims=((1,), (0,))):
        return lax.dot_general(a, b, (dims, ((), ())), preferred_element_type=jnp.float32)

    within = dot(ones, ahead(rows))
    totals = dot(jnp.ones((8, rows), jnp.bfloat16), ones, ((1,), (1,)))
    first = dot(totals.astype(jnp.bfloat16), ahead(blocks))
    offs_ref[...] = first.astype(jnp.int32)
    wide = jnp.broadcast_to(jnp.sum(ones.astype(jnp.float32), axis=1, keepdims=True), (blocks, rows))
    before = dot(ahead(blocks), wide.astype(jnp.bfloat16), ((0,), (0,)))
    pos_ref[...] = jnp.where(quality > 0, (before + within).astype(jnp.int32), -1)


def window(offs_ref, block):
    return pl.multiple_of((offs_ref[0, block] // ALIGN) * ALIGN, ALIGN)


def kept_rows(pos, start, tile):
    rows = tile.shape[0]
    at = lax.broadcasted_iota(jnp.int32, (rows + ALIGN, rows), 0) + start
    chosen = jnp.where(at == pos, 1.0, 0.0).astype(jnp.bfloat16)
    return jnp.dot(chosen, tile, preferred_element_type=jnp.float32).astype(jnp.bfloat16)


def put_rows(packed, start, part):
    rest = part.shape[0] - ALIGN
    packed[pl.ds(start, ALIGN), :] = packed[pl.ds(start, ALIGN), :] + part[:ALIGN]
    packed[pl.ds(pl.multiple_of(start + ALIGN, ALIGN), rest), :] = part[ALIGN:]


def clear(ref, start):
    def body(i, carry):
        at = pl.multiple_of(i * ALIGN, ALIGN)
        ref[pl.ds(at, ALIGN), :] = jnp.zeros((ALIGN, ref.shape[1]), ref.dtype)
        return carry

    lax.fori_loop(start // ALIGN, ref.shape[0] // ALIGN, body, 0)


def send_ready(packed, outs, sems, me, before, now, last):
    count = len(outs)
    size = outs[0].shape[0]
    for shift, copy in enumerate(part_copies(packed, outs, sems, me, True)):
        past = (lax.rem(me + shift, count) + 1) * size

        @pl.when((past > before) & ((past <= now) | last))
        def _():
            copy.start()


def group_copies(source, target, sems):
    pieces = sems.shape[0]
    size = source.shape[0] // pieces
    return [
        pltpu.make_async_copy(
            source.at[pl.ds(i * size, size)], target.at[pl.ds(i * size, size)], sems.at[i]
        )
        for i in range(pieces)
    ]


def group_wait(source, target, sems, i):
    size = source.shape[0] // sems.shape[0]
    pltpu.make_async_copy(
        source.at[pl.ds(0, size)], target.at[pl.ds(0, size)], sems.at[i]
    ).wait()


def pack_round(step, rounds, pos, offs, tiles, packed, outs, sems, me):
    found = []
    for i, tile in enumerate(tiles):
        start = window(offs, step * GROUP + i * PAIR)
        row = jnp.concatenate([pos[i * PAIR + j : i * PAIR + j + 1, :] for j in range(PAIR)], axis=1)
        found.append((start, kept_rows(row, start, tile)))
    for start, part in found:
        put_rows(packed, start, part)
    last = step == rounds - 1

    @pl.when(last)
    def _():
        start, part = found[-1]
        clear(packed, start + part.shape[0])

    before = jnp.where(step == 0, 0, window(offs, step * GROUP))
    now = window(offs, jnp.where(last, 0, (step + 1) * GROUP))
    send_ready(packed, outs, sems, me, before, now, last)


def part_copies(packed, parts, sems, me, outward):
    count = len(parts)
    size = parts[0].shape[0]
    copies = []
    for shift, part in enumerate(parts):
        owner = lax.rem(me + (shift if outward else count - shift), count)
        where = packed.at[pl.ds(pl.multiple_of(owner * size, ALIGN), size), :]
        ends = (where, part) if outward else (part, where)
        copies.append(pltpu.make_async_copy(*ends, sems.at[shift]))
    return copies


def compact_kernel(me_ref, quality_ref, v_ref, pos_ref, offs_ref, *rest):
    outs, (tiles, packed, sems, in_sems, offs, offs_sem) = rest[:-6], rest[-6:]
    nblk, block_rows = pos_ref.shape
    rounds = nblk // GROUP
    for copy in group_copies(v_ref, tiles, in_sems):
        copy.start()
    plan(quality_ref[...], pos_ref, offs_ref)
    copy = pltpu.make_async_copy(offs_ref, offs, offs_sem)
    copy.start()
    packed[:ALIGN, :] = jnp.zeros((ALIGN, packed.shape[1]), packed.dtype)
    copy.wait()

    def body(step, carry):
        group_wait(v_ref, tiles, in_sems, step)
        pos = pos_ref[pl.ds(pl.multiple_of(step * GROUP, GROUP), GROUP), :]
        span = PAIR * block_rows
        made = []
        for i in range(GROUP // PAIR):
            at = pl.multiple_of(step * (GROUP * block_rows) + i * span, span)
            made.append(tiles[pl.ds(at, span), :])
        pack_round(step, rounds, pos, offs, made, packed, outs, sems, me_ref[0])
        return carry

    lax.fori_loop(0, rounds, body, 0)
    for copy in part_copies(packed, outs, sems, me_ref[0], True):
        copy.wait()


def part_shapes(size, count, width):
    return (jax.ShapeDtypeStruct((size, width), jnp.bfloat16),) * count


def compact(v, quality, me, size, count):
    rows, width = v.shape
    nblk, block_rows = quality.shape
    shapes = part_shapes(size, count, width)
    plan_shapes = (
        jax.ShapeDtypeStruct((nblk, block_rows), jnp.int32),
        jax.ShapeDtypeStruct((8, nblk), jnp.int32),
    )
    pos, offs, *parts = pl.pallas_call(
        compact_kernel,
        out_shape=plan_shapes + shapes,
        grid_spec=pltpu.PrefetchScalarGridSpec(
            num_scalar_prefetch=1,
            grid=(1,),
            in_specs=[
                pl.BlockSpec((nblk, block_rows), lambda i, *_: (0, 0)),
                pl.BlockSpec(memory_space=pl.ANY),
            ],
            out_specs=[
                pl.BlockSpec((nblk, block_rows), lambda i, *_: (0, 0)),
                pl.BlockSpec((8, nblk), lambda i, *_: (0, 0)),
            ]
            + [pl.BlockSpec(memory_space=pl.ANY)] * len(shapes),
            scratch_shapes=[
                pltpu.VMEM((rows, width), jnp.bfloat16),
                pltpu.VMEM((rows + ALIGN, width), jnp.bfloat16),
                pltpu.SemaphoreType.DMA((len(shapes),)),
                pltpu.SemaphoreType.DMA((nblk // GROUP,)),
                pltpu.SMEM((8, nblk), jnp.int32),
                pltpu.SemaphoreType.DMA,
            ],
        ),
        compiler_params=params(),
        cost_estimate=pl.CostEstimate(
            flops=2 * rows * 272 * width, bytes_accessed=4 * rows * width, transcendentals=0
        ),
    )(me, quality, v)
    return pos, offs, tuple(parts)


def expand_kernel(me_ref, offs_ref, pos_ref, *rest):
    ins, (out_ref, packed, tiles, sems, out_sems) = rest[:-5], rest[-5:]
    nblk, block_rows = pos_ref.shape
    rounds = nblk // GROUP
    span = EXPAND * block_rows
    held = len(ins) * ins[0].shape[0]
    copies = part_copies(packed, ins, sems, me_ref[0], False)
    for copy in copies:
        copy.start()
    clear(packed, held)
    for copy in copies:
        copy.wait()

    def body(step, carry):
        pos = pos_ref[pl.ds(pl.multiple_of(step * GROUP, GROUP), GROUP), :]
        made = []
        for i in range(0, GROUP, EXPAND):
            start = window(offs_ref, step * GROUP + i)
            row = jnp.concatenate([pos[i + j : i + j + 1, :] for j in range(EXPAND)], axis=1)
            at = lax.broadcasted_iota(jnp.int32, (span + ALIGN, span), 0) + start
            chosen = jnp.where(at == row, 1.0, 0.0).astype(jnp.bfloat16)
            made.append(
                lax.dot_general(
                    chosen,
                    packed[pl.ds(start, span + ALIGN), :],
                    (((0,), (0,)), ((), ())),
                    preferred_element_type=jnp.float32,
                ).astype(jnp.bfloat16)
            )
        size = GROUP * block_rows
        base = pl.multiple_of(step * size, size)
        for i, rows in enumerate(made):
            tiles[pl.ds(pl.multiple_of(base + i * span, span), span), :] = rows
        pltpu.make_async_copy(
            tiles.at[pl.ds(base, size)], out_ref.at[pl.ds(base, size)], out_sems.at[step]
        ).start()
        return carry

    lax.fori_loop(0, rounds, body, 0)
    for copy in group_copies(tiles, out_ref, out_sems):
        copy.wait()


def expand(parts, pos, offs, me):
    nblk, block_rows = pos.shape
    rows = nblk * block_rows
    width = parts[0].shape[1]
    return pl.pallas_call(
        expand_kernel,
        out_shape=jax.ShapeDtypeStruct((rows, width), jnp.bfloat16),
        grid_spec=pltpu.PrefetchScalarGridSpec(
            num_scalar_prefetch=2,
            grid=(1,),
            in_specs=[pl.BlockSpec((nblk, block_rows), lambda i, *_: (0, 0))]
            + [pl.BlockSpec(memory_space=pl.ANY)] * len(parts),
            out_specs=pl.BlockSpec(memory_space=pl.ANY),
            scratch_shapes=[
                pltpu.VMEM((rows + ALIGN, width), jnp.bfloat16),
                pltpu.VMEM((rows, width), jnp.bfloat16),
                pltpu.SemaphoreType.DMA((len(parts),)),
                pltpu.SemaphoreType.DMA((nblk // GROUP,)),
            ],
        ),
        compiler_params=params(),
        cost_estimate=pl.CostEstimate(
            flops=2 * rows * 256 * width, bytes_accessed=4 * rows * width, transcendentals=0
        ),
    )(me, offs, pos, *parts)


def spatial_kernel(
    compacting, me_ref, offs_ref, ids_ref, counts_ref, pos_ref, weight_ref, near, own, far, *rest
):
    nblk, block_rows = pos_ref.shape
    slots = weight_ref.shape[1]
    rounds = nblk // GROUP
    scratch = 6
    outs, (tiles, weights, halo_sems, weight_sems, made, sems) = rest[:-scratch], rest[-scratch:]
    rows = tiles.shape[0] // 3
    loads = group_copies(weight_ref, weights, weight_sems)
    loads[0].start()
    halo = [
        pltpu.make_async_copy(source, tiles.at[pl.ds(i * rows, rows), :], halo_sems.at[i])
        for i, source in enumerate((near, own, far))
    ]
    for copy in halo + loads[1:]:
        copy.start()
    if compacting:
        made[:ALIGN, :] = jnp.zeros((ALIGN, made.shape[1]), made.dtype)
    for copy in halo:
        copy.wait()

    def product(step, i):
        block = step * GROUP + i
        used = counts_ref[block]
        live = []
        picked = []
        for slot in range(slots):
            at = ids_ref[block * slots + slot]
            scale = jnp.where(slot < used, 1.0, 0.0).astype(jnp.bfloat16)
            live.append(weights[block, slot] * scale)
            start = pl.multiple_of(at * block_rows, block_rows)
            picked.append(tiles[pl.ds(start, block_rows), :])
        return jnp.dot(
            jnp.concatenate(live, axis=1),
            jnp.concatenate(picked, axis=0),
            preferred_element_type=jnp.float32,
        ).astype(jnp.bfloat16)

    def body(step, carry):
        group_wait(weight_ref, weights, weight_sems, step)
        pos = pos_ref[pl.ds(pl.multiple_of(step * GROUP, GROUP), GROUP), :]
        found = [product(step, i) for i in range(GROUP)]
        if compacting:
            found = [
                jnp.concatenate(found[i : i + PAIR], axis=0) for i in range(0, GROUP, PAIR)
            ]
            pack_round(step, rounds, pos, offs_ref, found, made, outs, sems, me_ref[0])
            return carry
        a = lax.broadcasted_iota(jnp.int32, (block_rows, block_rows), 0)
        b = lax.broadcasted_iota(jnp.int32, (block_rows, block_rows), 1)
        size = GROUP * block_rows
        base = pl.multiple_of(step * size, size)
        for i in range(GROUP):
            kept = jnp.where((a == b) & (pos[i : i + 1, :] >= 0), 1.0, 0.0).astype(jnp.bfloat16)
            made[pl.ds(pl.multiple_of(base + i * block_rows, block_rows), block_rows), :] = jnp.dot(
                kept, found[i], preferred_element_type=jnp.float32
            ).astype(jnp.bfloat16)
        pltpu.make_async_copy(
            made.at[pl.ds(base, size)], outs[0].at[pl.ds(base, size)], sems.at[step]
        ).start()
        return carry

    lax.fori_loop(0, rounds, body, 0)
    if compacting:
        copies = part_copies(made, outs, sems, me_ref[0], True)
    else:
        copies = group_copies(made, outs[0], sems)
    for copy in copies:
        copy.wait()


def spatial(halo, weights, ids, counts, pos, offs, me, size, count):
    rows, width = halo[1].shape
    nblk, block_rows = pos.shape
    slots = weights.shape[1]
    any_spec = pl.BlockSpec(memory_space=pl.ANY)
    rounds = nblk // GROUP
    if size is None:
        shapes = (jax.ShapeDtypeStruct((rows, width), jnp.bfloat16),)
        made = (rows, rounds)
    else:
        shapes = part_shapes(size, count, width)
        made = (rows + ALIGN, len(shapes))
    return pl.pallas_call(
        functools.partial(spatial_kernel, size is not None),
        out_shape=shapes,
        grid_spec=pltpu.PrefetchScalarGridSpec(
            num_scalar_prefetch=4,
            grid=(1,),
            in_specs=[pl.BlockSpec((nblk, block_rows), lambda i, *_: (0, 0))] + [any_spec] * 4,
            out_specs=[any_spec] * len(shapes),
            scratch_shapes=[
                pltpu.VMEM((3 * rows, width), jnp.bfloat16),
                pltpu.VMEM(weights.shape, jnp.bfloat16),
                pltpu.SemaphoreType.DMA((3,)),
                pltpu.SemaphoreType.DMA((rounds,)),
                pltpu.VMEM((made[0], width), jnp.bfloat16),
                pltpu.SemaphoreType.DMA((made[1],)),
            ],
        ),
        compiler_params=params(),
        cost_estimate=pl.CostEstimate(
            flops=2 * rows * slots * block_rows * width,
            bytes_accessed=8 * rows * width + 2 * rows * slots * block_rows,
            transcendentals=0,
        ),
    )(me, offs, ids, counts, pos, weights, *halo)


def mix_kernel(count, me_ref, op_ref, *rest):
    ins, outs, (rolled, sems) = rest[:count], rest[count : 2 * count], rest[2 * count :]
    width = ins[0].shape[1]
    me = me_ref[0]

    @pl.when(pl.program_id(0) == 0)
    def _():
        copies = []
        for shift in range(count):
            source = lax.rem(me + count - shift, count)
            copies.append(
                pltpu.make_async_copy(
                    op_ref.at[pl.ds(pl.multiple_of(source * width, ALIGN), width), :],
                    rolled.at[pl.ds(shift * width, width), :],
                    sems.at[shift],
                )
            )
        for copy in copies:
            copy.start()
        for copy in copies:
            copy.wait()

    row = jnp.concatenate([part[...] for part in ins], axis=1)
    for shift in range(count):
        dest = lax.rem(me + shift, count)
        columns = rolled[:, pl.ds(pl.multiple_of(dest * width, 128), width)]
        outs[shift][...] = jnp.dot(row, columns, preferred_element_type=jnp.float32).astype(
            jnp.bfloat16
        )


def mix(parts, chan_op, me):
    count = len(parts)
    rows, width = parts[0].shape
    tiles = [t for t in range(ALIGN, min(rows, 640) + 1, ALIGN) if rows % t == 0]
    tile = tiles[-1]
    spec = pl.BlockSpec((tile, width), lambda i, *_: (i, 0))
    return pl.pallas_call(
        functools.partial(mix_kernel, count),
        out_shape=part_shapes(rows, count, width),
        grid_spec=pltpu.PrefetchScalarGridSpec(
            num_scalar_prefetch=1,
            grid=(rows // tile,),
            in_specs=[pl.BlockSpec(memory_space=pl.ANY)] + [spec] * count,
            out_specs=[spec] * count,
            scratch_shapes=[
                pltpu.VMEM(chan_op.shape, jnp.bfloat16),
                pltpu.SemaphoreType.DMA((count,)),
            ],
        ),
        compiler_params=params(),
        cost_estimate=pl.CostEstimate(flops=1, bytes_accessed=1, transcendentals=0),
    )(me, chan_op, *parts)


class Line:
    def __init__(self, depth):
        self.depth = depth
        self.done = []

    def exchange(self, parts):
        count = len(parts)
        arrived = list(parts)
        for shift in sorted(range(1, count), key=lambda k: min(k, count - k)):
            part = parts[shift]
            if len(self.done) >= self.depth:
                part = after(part, self.done[-self.depth])
            arrived[shift] = lax.ppermute(
                part, "chan", [(i, (i + shift) % count) for i in range(count)]
            )
            self.done.append(arrived[shift])
        return tuple(arrived)


def after(values, *others):
    return lax.optimization_barrier((values, others))[0]


def halo_of(x):
    count = lax.axis_size("orbit")
    far = [(i, i + 1) for i in range(1, count - 1, 2)]
    far = lax.ppermute(x, "orbit", far + [(b, a) for a, b in far])
    near = [(i, i + 1) for i in range(0, count - 1, 2)]
    near = lax.ppermute(x, "orbit", near + [(b, a) for a, b in near])
    return near, x, far


def halo_ids(neighbours, nblk):
    mine = lax.axis_index("orbit")
    local = jnp.clip(neighbours - (mine - 1) * nblk, 0, 3 * nblk - 1)
    side = local // nblk
    side = jnp.where(mine % 2 == 0, 2 - side, side)
    return (side * nblk + local % nblk).reshape(-1)


def weigh(
    innovation, perturbation, quality, neighbours, counts, spatial_blocks, chan_op, capacity, watch
):
    rows, width = innovation.shape
    block_rows = spatial_blocks.shape[2]
    nblk = rows // block_rows
    count = lax.axis_size("chan")
    size = capacity // count

    me = lax.axis_index("chan").astype(jnp.int32).reshape(1)
    ids = halo_ids(neighbours, nblk)

    def spread(halo, room):
        return spatial(halo, spatial_blocks, ids, counts, pos, offs, me, room, count)

    kept = quality.reshape(nblk, block_rows)
    pos, offs, parts_i = compact(innovation, kept, me, size, count)
    line = Line(DEPTH)
    there_i = line.exchange(parts_i)
    perturbation, quality = after((perturbation, quality), parts_i[0])
    masked_p = perturbation * quality.astype(jnp.bfloat16)[:, None]
    parts_p = spread(halo_of(masked_p), size)
    there_p = line.exchange(parts_p)

    mixed_i = mix(after(there_i, parts_p[0]), chan_op, me)
    back_i = line.exchange(mixed_i)
    mixed_p = mix(after(there_p, mixed_i[0]), chan_op, me)
    back_p = line.exchange(mixed_p)
    seen = watch(after(quality, mixed_p[0]))

    wide_i = expand(after(back_i, mixed_p[0]), pos, offs, me)
    (out_i,) = spread(halo_of(wide_i), None)
    out_p = expand(after(back_p, out_i), pos, offs, me)
    return (out_i, out_p), seen


def shards(innovation, perturbation, quality, *others):
    rows = innovation.shape[0]
    unit = ALIGN * lax.axis_size("chan")
    capacity = -(-rows * 57 // (64 * unit)) * unit
    given = (innovation, perturbation, quality, *others)

    def overfull(quality):
        more = jnp.sum(quality, dtype=jnp.int32) > capacity
        return lax.pmax(more.astype(jnp.int32), ("grp", "orbit"))

    packed, more = weigh(*given, capacity, overfull)
    return lax.cond(
        more > 0,
        lambda given, packed: weigh(*given, rows, lambda quality: None)[0],
        lambda given, packed: packed,
        given,
        packed,
    )


def solution(mesh):
    placed = (
        P(("grp", "orbit"), "chan"),
        P(("grp", "orbit"), "chan"),
        P(("grp", "orbit")),
        P(("grp", "orbit"), None),
        P(("grp", "orbit")),
        P(("grp", "orbit"), None, None, None),
        P(),
    )
    return jax.shard_map(
        shards,
        mesh=mesh,
        in_specs=placed,
        out_specs=(P(("grp", "orbit"), "chan"), P(("grp", "orbit"), "chan")),
        check_vma=False,
    )
```

```python
import functools

import jax
import jax.numpy as jnp
from jax import lax
from jax.experimental import pallas as pl
from jax.experimental.pallas import tpu as pltpu
from jax.sharding import PartitionSpec as P

MIB = 1024 * 1024
ALIGN = 16
DEPTH = 3
PAIR = 2
EXPAND = 1
GROUP = 8


def params(mib):
    return pltpu.CompilerParams(
        dimension_semantics=("arbitrary",), vmem_limit_bytes=mib * MIB
    )


def plan(quality, pos_ref, offs_ref):
    blocks, rows = quality.shape
    ones = quality.astype(jnp.float32).astype(jnp.bfloat16)

    def ahead(size):
        a = lax.broadcasted_iota(jnp.int32, (size, size), 0)
        b = lax.broadcasted_iota(jnp.int32, (size, size), 1)
        return jnp.where(a < b, 1.0, 0.0).astype(jnp.bfloat16)

    def dot(a, b, dims=((1,), (0,))):
        return lax.dot_general(a, b, (dims, ((), ())), preferred_element_type=jnp.float32)

    within = dot(ones, ahead(rows))
    totals = dot(jnp.ones((8, rows), jnp.bfloat16), ones, ((1,), (1,)))
    first = dot(totals.astype(jnp.bfloat16), ahead(blocks))
    offs_ref[...] = first.astype(jnp.int32)
    wide = jnp.broadcast_to(jnp.sum(ones.astype(jnp.float32), axis=1, keepdims=True), (blocks, rows))
    before = dot(ahead(blocks), wide.astype(jnp.bfloat16), ((0,), (0,)))
    pos_ref[...] = jnp.where(quality > 0, (before + within).astype(jnp.int32), -1)


def window(offs_ref, block):
    return pl.multiple_of((offs_ref[0, block] // ALIGN) * ALIGN, ALIGN)


def kept_rows(pos, start, tile):
    rows = tile.shape[0]
    at = lax.broadcasted_iota(jnp.int32, (rows + ALIGN, rows), 0) + start
    chosen = jnp.where(at == pos, 1.0, 0.0).astype(jnp.bfloat16)
    return jnp.dot(chosen, tile, preferred_element_type=jnp.float32).astype(jnp.bfloat16)


def put_rows(packed, start, part):
    rest = part.shape[0] - ALIGN
    packed[pl.ds(start, ALIGN), :] = packed[pl.ds(start, ALIGN), :] + part[:ALIGN]
    packed[pl.ds(pl.multiple_of(start + ALIGN, ALIGN), rest), :] = part[ALIGN:]


def clear(ref, start):
    def body(i, carry):
        at = pl.multiple_of(i * ALIGN, ALIGN)
        ref[pl.ds(at, ALIGN), :] = jnp.zeros((ALIGN, ref.shape[1]), ref.dtype)
        return carry

    lax.fori_loop(start // ALIGN, ref.shape[0] // ALIGN, body, 0)


def send_ready(packed, outs, sems, me, before, now, last):
    count = len(outs)
    size = outs[0].shape[0]
    for shift, copy in enumerate(part_copies(packed, outs, sems, me, True)):
        past = (lax.rem(me + shift, count) + 1) * size

        @pl.when((past > before) & ((past <= now) | last))
        def _():
            copy.start()


def group_copies(source, target, sems):
    pieces = sems.shape[0]
    size = source.shape[0] // pieces
    return [
        pltpu.make_async_copy(
            source.at[pl.ds(i * size, size)], target.at[pl.ds(i * size, size)], sems.at[i]
        )
        for i in range(pieces)
    ]


def group_wait(source, target, sems, i):
    size = source.shape[0] // sems.shape[0]
    pltpu.make_async_copy(
        source.at[pl.ds(0, size)], target.at[pl.ds(0, size)], sems.at[i]
    ).wait()


def pack_round(step, rounds, pos, offs, tiles, packed, outs, sems, me):
    found = []
    for i, tile in enumerate(tiles):
        start = window(offs, step * GROUP + i * PAIR)
        row = jnp.concatenate([pos[i * PAIR + j : i * PAIR + j + 1, :] for j in range(PAIR)], axis=1)
        found.append((start, kept_rows(row, start, tile)))
    for start, part in found:
        put_rows(packed, start, part)
    last = step == rounds - 1

    @pl.when(last)
    def _():
        start, part = found[-1]
        clear(packed, start + part.shape[0])

    before = jnp.where(step == 0, 0, window(offs, step * GROUP))
    now = window(offs, jnp.where(last, 0, (step + 1) * GROUP))
    send_ready(packed, outs, sems, me, before, now, last)


def part_copies(packed, parts, sems, me, outward):
    count = len(parts)
    size = parts[0].shape[0]
    copies = []
    for shift, part in enumerate(parts):
        owner = lax.rem(me + (shift if outward else count - shift), count)
        where = packed.at[pl.ds(pl.multiple_of(owner * size, ALIGN), size), :]
        ends = (where, part) if outward else (part, where)
        copies.append(pltpu.make_async_copy(*ends, sems.at[shift]))
    return copies


def compact_kernel(me_ref, quality_ref, v_ref, pos_ref, offs_ref, *rest):
    outs, (tiles, packed, sems, in_sems, offs, offs_sem) = rest[:-6], rest[-6:]
    nblk, block_rows = pos_ref.shape
    rounds = nblk // GROUP
    for copy in group_copies(v_ref, tiles, in_sems):
        copy.start()
    plan(quality_ref[...], pos_ref, offs_ref)
    copy = pltpu.make_async_copy(offs_ref, offs, offs_sem)
    copy.start()
    packed[:ALIGN, :] = jnp.zeros((ALIGN, packed.shape[1]), packed.dtype)
    copy.wait()

    def body(step, carry):
        group_wait(v_ref, tiles, in_sems, step)
        pos = pos_ref[pl.ds(pl.multiple_of(step * GROUP, GROUP), GROUP), :]
        span = PAIR * block_rows
        made = []
        for i in range(GROUP // PAIR):
            at = pl.multiple_of(step * (GROUP * block_rows) + i * span, span)
            made.append(tiles[pl.ds(at, span), :])
        pack_round(step, rounds, pos, offs, made, packed, outs, sems, me_ref[0])
        return carry

    lax.fori_loop(0, rounds, body, 0)
    for copy in part_copies(packed, outs, sems, me_ref[0], True):
        copy.wait()


def part_shapes(size, count, width):
    return (jax.ShapeDtypeStruct((size, width), jnp.bfloat16),) * count


def compact(v, quality, me, size, count):
    rows, width = v.shape
    nblk, block_rows = quality.shape
    shapes = part_shapes(size, count, width)
    plan_shapes = (
        jax.ShapeDtypeStruct((nblk, block_rows), jnp.int32),
        jax.ShapeDtypeStruct((8, nblk), jnp.int32),
    )
    pos, offs, *parts = pl.pallas_call(
        compact_kernel,
        out_shape=plan_shapes + shapes,
        grid_spec=pltpu.PrefetchScalarGridSpec(
            num_scalar_prefetch=1,
            grid=(1,),
            in_specs=[
                pl.BlockSpec((nblk, block_rows), lambda i, *_: (0, 0)),
                pl.BlockSpec(memory_space=pl.ANY),
            ],
            out_specs=[
                pl.BlockSpec((nblk, block_rows), lambda i, *_: (0, 0)),
                pl.BlockSpec((8, nblk), lambda i, *_: (0, 0)),
            ]
            + [pl.BlockSpec(memory_space=pl.ANY)] * len(shapes),
            scratch_shapes=[
                pltpu.VMEM((rows, width), jnp.bfloat16),
                pltpu.VMEM((rows + ALIGN, width), jnp.bfloat16),
                pltpu.SemaphoreType.DMA((len(shapes),)),
                pltpu.SemaphoreType.DMA((nblk // GROUP,)),
                pltpu.SMEM((8, nblk), jnp.int32),
                pltpu.SemaphoreType.DMA,
            ],
        ),
        compiler_params=params(16),
        cost_estimate=pl.CostEstimate(
            flops=2 * rows * 272 * width, bytes_accessed=4 * rows * width, transcendentals=0
        ),
    )(me, quality, v)
    return pos, offs, tuple(parts)


def expand_kernel(me_ref, offs_ref, pos_ref, *rest):
    ins, (out_ref, packed, tiles, sems, out_sems) = rest[:-5], rest[-5:]
    nblk, block_rows = pos_ref.shape
    rounds = nblk // GROUP
    span = EXPAND * block_rows
    held = len(ins) * ins[0].shape[0]
    copies = part_copies(packed, ins, sems, me_ref[0], False)
    for copy in copies:
        copy.start()
    clear(packed, held)
    for copy in copies:
        copy.wait()

    def body(step, carry):
        pos = pos_ref[pl.ds(pl.multiple_of(step * GROUP, GROUP), GROUP), :]
        made = []
        for i in range(0, GROUP, EXPAND):
            start = window(offs_ref, step * GROUP + i)
            row = jnp.concatenate([pos[i + j : i + j + 1, :] for j in range(EXPAND)], axis=1)
            at = lax.broadcasted_iota(jnp.int32, (span + ALIGN, span), 0) + start
            chosen = jnp.where(at == row, 1.0, 0.0).astype(jnp.bfloat16)
            made.append(
                lax.dot_general(
                    chosen,
                    packed[pl.ds(start, span + ALIGN), :],
                    (((0,), (0,)), ((), ())),
                    preferred_element_type=jnp.float32,
                ).astype(jnp.bfloat16)
            )
        size = GROUP * block_rows
        base = pl.multiple_of(step * size, size)
        for i, rows in enumerate(made):
            tiles[pl.ds(pl.multiple_of(base + i * span, span), span), :] = rows
        pltpu.make_async_copy(
            tiles.at[pl.ds(base, size)], out_ref.at[pl.ds(base, size)], out_sems.at[step]
        ).start()
        return carry

    lax.fori_loop(0, rounds, body, 0)
    for copy in group_copies(tiles, out_ref, out_sems):
        copy.wait()


def expand(parts, pos, offs, me):
    nblk, block_rows = pos.shape
    rows = nblk * block_rows
    width = parts[0].shape[1]
    return pl.pallas_call(
        expand_kernel,
        out_shape=jax.ShapeDtypeStruct((rows, width), jnp.bfloat16),
        grid_spec=pltpu.PrefetchScalarGridSpec(
            num_scalar_prefetch=2,
            grid=(1,),
            in_specs=[pl.BlockSpec((nblk, block_rows), lambda i, *_: (0, 0))]
            + [pl.BlockSpec(memory_space=pl.ANY)] * len(parts),
            out_specs=pl.BlockSpec(memory_space=pl.ANY),
            scratch_shapes=[
                pltpu.VMEM((rows + ALIGN, width), jnp.bfloat16),
                pltpu.VMEM((rows, width), jnp.bfloat16),
                pltpu.SemaphoreType.DMA((len(parts),)),
                pltpu.SemaphoreType.DMA((nblk // GROUP,)),
            ],
        ),
        compiler_params=params(16),
        cost_estimate=pl.CostEstimate(
            flops=2 * rows * 256 * width, bytes_accessed=4 * rows * width, transcendentals=0
        ),
    )(me, offs, pos, *parts)


def spatial_kernel(
    compacting, me_ref, offs_ref, ids_ref, counts_ref, pos_ref, weight_ref, near, own, far, _, *rest
):
    nblk, block_rows = pos_ref.shape
    slots = weight_ref.shape[1]
    rounds = nblk // GROUP
    scratch = 6
    outs, (tiles, weights, halo_sems, weight_sems, made, sems) = rest[:-scratch], rest[-scratch:]
    rows = tiles.shape[0] // 3
    loads = group_copies(weight_ref, weights, weight_sems)
    loads[0].start()
    halo = [
        pltpu.make_async_copy(source, tiles.at[pl.ds(i * rows, rows), :], halo_sems.at[i])
        for i, source in enumerate((near, own, far))
    ]
    for copy in halo + loads[1:]:
        copy.start()
    if compacting:
        made[:ALIGN, :] = jnp.zeros((ALIGN, made.shape[1]), made.dtype)
    for copy in halo:
        copy.wait()

    def product(step, i):
        block = step * GROUP + i
        used = counts_ref[block]
        live = []
        picked = []
        for slot in range(slots):
            at = ids_ref[block * slots + slot]
            scale = jnp.where(slot < used, 1.0, 0.0).astype(jnp.bfloat16)
            live.append(weights[block, slot] * scale)
            start = pl.multiple_of(at * block_rows, block_rows)
            picked.append(tiles[pl.ds(start, block_rows), :])
        return jnp.dot(
            jnp.concatenate(live, axis=1),
            jnp.concatenate(picked, axis=0),
            preferred_element_type=jnp.float32,
        ).astype(jnp.bfloat16)

    def body(step, carry):
        group_wait(weight_ref, weights, weight_sems, step)
        pos = pos_ref[pl.ds(pl.multiple_of(step * GROUP, GROUP), GROUP), :]
        found = [product(step, i) for i in range(GROUP)]
        if compacting:
            found = [
                jnp.concatenate(found[i : i + PAIR], axis=0) for i in range(0, GROUP, PAIR)
            ]
            pack_round(step, rounds, pos, offs_ref, found, made, outs, sems, me_ref[0])
            return carry
        a = lax.broadcasted_iota(jnp.int32, (block_rows, block_rows), 0)
        b = lax.broadcasted_iota(jnp.int32, (block_rows, block_rows), 1)
        size = GROUP * block_rows
        base = pl.multiple_of(step * size, size)
        for i in range(GROUP):
            kept = jnp.where((a == b) & (pos[i : i + 1, :] >= 0), 1.0, 0.0).astype(jnp.bfloat16)
            made[pl.ds(pl.multiple_of(base + i * block_rows, block_rows), block_rows), :] = jnp.dot(
                kept, found[i], preferred_element_type=jnp.float32
            ).astype(jnp.bfloat16)
        pltpu.make_async_copy(
            made.at[pl.ds(base, size)], outs[0].at[pl.ds(base, size)], sems.at[step]
        ).start()
        return carry

    lax.fori_loop(0, rounds, body, 0)
    if compacting:
        copies = part_copies(made, outs, sems, me_ref[0], True)
    else:
        copies = group_copies(made, outs[0], sems)
    for copy in copies:
        copy.wait()


def spatial(halo, weights, ids, counts, pos, offs, me, size, count):
    rows, width = halo[1].shape
    nblk, block_rows = pos.shape
    slots = weights.shape[1]
    any_spec = pl.BlockSpec(memory_space=pl.ANY)
    rounds = nblk // GROUP
    if size is None:
        shapes = (jax.ShapeDtypeStruct((rows, width), jnp.bfloat16),)
        made = (rows, rounds)
    else:
        shapes = part_shapes(size, count, width)
        made = (rows + ALIGN, len(shapes))
    return pl.pallas_call(
        functools.partial(spatial_kernel, size is not None),
        out_shape=shapes,
        grid_spec=pltpu.PrefetchScalarGridSpec(
            num_scalar_prefetch=4,
            grid=(1,),
            in_specs=[pl.BlockSpec((nblk, block_rows), lambda i, *_: (0, 0))] + [any_spec] * 5,
            out_specs=[any_spec] * len(shapes),
            scratch_shapes=[
                pltpu.VMEM((3 * rows, width), jnp.bfloat16),
                pltpu.VMEM(weights.shape, jnp.bfloat16),
                pltpu.SemaphoreType.DMA((3,)),
                pltpu.SemaphoreType.DMA((rounds,)),
                pltpu.VMEM((made[0], width), jnp.bfloat16),
                pltpu.SemaphoreType.DMA((made[1],)),
            ],
        ),
        compiler_params=params(34),
        cost_estimate=pl.CostEstimate(
            flops=2 * rows * slots * block_rows * width,
            bytes_accessed=8 * rows * width + 2 * rows * slots * block_rows,
            transcendentals=0,
        ),
    )(me, offs, ids, counts, pos, weights, *halo)


def mix_kernel(count, me_ref, op_ref, *rest):
    ins, outs, (rolled, sems) = rest[:count], rest[count : 2 * count], rest[2 * count :]
    width = ins[0].shape[1]
    me = me_ref[0]

    @pl.when(pl.program_id(0) == 0)
    def _():
        copies = []
        for shift in range(count):
            source = lax.rem(me + count - shift, count)
            copies.append(
                pltpu.make_async_copy(
                    op_ref.at[pl.ds(pl.multiple_of(source * width, ALIGN), width), :],
                    rolled.at[pl.ds(shift * width, width), :],
                    sems.at[shift],
                )
            )
        for copy in copies:
            copy.start()
        for copy in copies:
            copy.wait()

    row = jnp.concatenate([part[...] for part in ins], axis=1)
    for shift in range(count):
        dest = lax.rem(me + shift, count)
        columns = rolled[:, pl.ds(pl.multiple_of(dest * width, 128), width)]
        outs[shift][...] = jnp.dot(row, columns, preferred_element_type=jnp.float32).astype(
            jnp.bfloat16
        )


def mix(parts, chan_op, me):
    count = len(parts)
    rows, width = parts[0].shape
    tiles = [t for t in range(ALIGN, min(rows, 640) + 1, ALIGN) if rows % t == 0]
    tile = tiles[-1]
    spec = pl.BlockSpec((tile, width), lambda i, *_: (i, 0))
    return pl.pallas_call(
        functools.partial(mix_kernel, count),
        out_shape=part_shapes(rows, count, width),
        grid_spec=pltpu.PrefetchScalarGridSpec(
            num_scalar_prefetch=1,
            grid=(rows // tile,),
            in_specs=[pl.BlockSpec(memory_space=pl.ANY)] + [spec] * count,
            out_specs=[spec] * count,
            scratch_shapes=[
                pltpu.VMEM(chan_op.shape, jnp.bfloat16),
                pltpu.SemaphoreType.DMA((count,)),
            ],
        ),
        compiler_params=params(16),
        cost_estimate=pl.CostEstimate(flops=1, bytes_accessed=1, transcendentals=0),
    )(me, chan_op, *parts)


class Line:
    def __init__(self, depth):
        self.depth = depth
        self.done = []

    def exchange(self, parts):
        count = len(parts)
        arrived = list(parts)
        for shift in sorted(range(1, count), key=lambda k: min(k, count - k)):
            part = parts[shift]
            if len(self.done) >= self.depth:
                part = after(part, self.done[-self.depth])
            arrived[shift] = lax.ppermute(
                part, "chan", [(i, (i + shift) % count) for i in range(count)]
            )
            self.done.append(arrived[shift])
        return tuple(arrived)


def after(values, *others):
    return lax.optimization_barrier((values, others))[0]


def gate_kernel(x_ref, out_ref):
    out_ref[...] = x_ref[...]


def gate(x):
    shape = (ALIGN, x.shape[1])
    spec = pl.BlockSpec(shape, lambda i: (0, 0))
    return pl.pallas_call(
        gate_kernel,
        out_shape=jax.ShapeDtypeStruct(shape, x.dtype),
        grid=(1,),
        in_specs=[spec],
        out_specs=spec,
        cost_estimate=pl.CostEstimate(flops=10**11, bytes_accessed=1, transcendentals=0),
    )(x)


def halo_of(x):
    count = lax.axis_size("orbit")
    far = [(i, i + 1) for i in range(1, count - 1, 2)]
    far = lax.ppermute(x, "orbit", far + [(b, a) for a, b in far])
    near = [(i, i + 1) for i in range(0, count - 1, 2)]
    near = lax.ppermute(x, "orbit", near + [(b, a) for a, b in near])
    return near, x, far


def halo_ids(neighbours, nblk):
    mine = lax.axis_index("orbit")
    local = jnp.clip(neighbours - (mine - 1) * nblk, 0, 3 * nblk - 1)
    side = local // nblk
    side = jnp.where(mine % 2 == 0, 2 - side, side)
    return (side * nblk + local % nblk).reshape(-1)


def weigh(
    innovation, perturbation, quality, neighbours, counts, spatial_blocks, chan_op, capacity, watch
):
    rows, width = innovation.shape
    block_rows = spatial_blocks.shape[2]
    nblk = rows // block_rows
    count = lax.axis_size("chan")
    size = capacity // count

    me = lax.axis_index("chan").astype(jnp.int32).reshape(1)
    ids = halo_ids(neighbours, nblk)

    def spread(halo, room):
        return spatial(halo, spatial_blocks, ids, counts, pos, offs, me, room, count)

    kept = quality.reshape(nblk, block_rows)
    pos, offs, parts_i = compact(innovation, kept, me, size, count)
    line = Line(DEPTH)
    there_i = line.exchange(parts_i)
    perturbation, quality = after((perturbation, quality), parts_i[0])
    masked_p = perturbation * quality.astype(jnp.bfloat16)[:, None]
    parts_p = spread((*halo_of(masked_p), gate(there_i[1 % count])), size)
    there_p = line.exchange(parts_p)

    mixed_i = mix(after(there_i, parts_p[0]), chan_op, me)
    back_i = line.exchange(mixed_i)
    seen = watch(after(quality, parts_p[0]))
    mixed_p = mix(after(there_p, (mixed_i[0], seen)), chan_op, me)
    back_p = line.exchange(after(mixed_p, back_i))

    wide_i = expand(after(back_i, mixed_p[0]), pos, offs, me)
    (out_i,) = spread((*halo_of(wide_i), gate(back_p[count // 2])), None)
    out_p = expand(after(back_p, out_i), pos, offs, me)
    return (out_i, out_p), seen


def shards(innovation, perturbation, quality, *others):
    rows = innovation.shape[0]
    unit = ALIGN * lax.axis_size("chan")
    capacity = -(-rows * 57 // (64 * unit)) * unit
    given = (innovation, perturbation, quality, *others)

    def overfull(quality):
        more = jnp.sum(quality, dtype=jnp.int32) > capacity
        return lax.pmax(more.astype(jnp.int32), ("grp", "orbit"))

    packed, more = weigh(*given, capacity, overfull)
    return lax.cond(
        more > 0,
        lambda given, packed: weigh(*given, rows, lambda quality: None)[0],
        lambda given, packed: packed,
        given,
        packed,
    )


def solution(mesh):
    placed = (
        P(("grp", "orbit"), "chan"),
        P(("grp", "orbit"), "chan"),
        P(("grp", "orbit")),
        P(("grp", "orbit"), None),
        P(("grp", "orbit")),
        P(("grp", "orbit"), None, None, None),
        P(),
    )
    return jax.shard_map(
        shards,
        mesh=mesh,
        in_specs=placed,
        out_specs=(P(("grp", "orbit"), "chan"), P(("grp", "orbit"), "chan")),
        check_vma=False,
    )
```

```python
import functools

import jax
import jax.numpy as jnp
from jax import lax
from jax.experimental import pallas as pl
from jax.experimental.pallas import tpu as pltpu
from jax.sharding import PartitionSpec as P

MIB = 1024 * 1024
ALIGN = 16
DEPTH = 4
PAIR = 2
EXPAND = 1
GROUP = 16


def params(mib):
    return pltpu.CompilerParams(
        dimension_semantics=("arbitrary",), vmem_limit_bytes=mib * MIB
    )


def plan(quality, pos_ref, offs_ref):
    blocks, rows = quality.shape
    ones = quality.astype(jnp.float32).astype(jnp.bfloat16)

    def ahead(size):
        a = lax.broadcasted_iota(jnp.int32, (size, size), 0)
        b = lax.broadcasted_iota(jnp.int32, (size, size), 1)
        return jnp.where(a < b, 1.0, 0.0).astype(jnp.bfloat16)

    def dot(a, b, dims=((1,), (0,))):
        return lax.dot_general(a, b, (dims, ((), ())), preferred_element_type=jnp.float32)

    within = dot(ones, ahead(rows))
    totals = dot(jnp.ones((8, rows), jnp.bfloat16), ones, ((1,), (1,)))
    first = dot(totals.astype(jnp.bfloat16), ahead(blocks))
    offs_ref[...] = first.astype(jnp.int32)
    wide = jnp.broadcast_to(jnp.sum(ones.astype(jnp.float32), axis=1, keepdims=True), (blocks, rows))
    before = dot(ahead(blocks), wide.astype(jnp.bfloat16), ((0,), (0,)))
    pos_ref[...] = jnp.where(quality > 0, (before + within).astype(jnp.int32), -1)


def window(offs_ref, block):
    return pl.multiple_of((offs_ref[0, block] // ALIGN) * ALIGN, ALIGN)


def kept_rows(pos, start, tile):
    rows = tile.shape[0]
    at = lax.broadcasted_iota(jnp.int32, (rows + ALIGN, rows), 0) + start
    chosen = jnp.where(at == pos, 1.0, 0.0).astype(jnp.bfloat16)
    return jnp.dot(chosen, tile, preferred_element_type=jnp.float32).astype(jnp.bfloat16)


def put_rows(packed, start, part):
    rest = part.shape[0] - ALIGN
    packed[pl.ds(start, ALIGN), :] = packed[pl.ds(start, ALIGN), :] + part[:ALIGN]
    packed[pl.ds(pl.multiple_of(start + ALIGN, ALIGN), rest), :] = part[ALIGN:]


def clear(ref, start):
    def body(i, carry):
        at = pl.multiple_of(i * ALIGN, ALIGN)
        ref[pl.ds(at, ALIGN), :] = jnp.zeros((ALIGN, ref.shape[1]), ref.dtype)
        return carry

    lax.fori_loop(start // ALIGN, ref.shape[0] // ALIGN, body, 0)


def send_ready(packed, outs, sems, me, before, now, last):
    count = len(outs)
    size = outs[0].shape[0]
    for shift, copy in enumerate(part_copies(packed, outs, sems, me, True)):
        past = (lax.rem(me + shift, count) + 1) * size

        @pl.when((past > before) & ((past <= now) | last))
        def _():
            copy.start()


def group_copies(source, target, sems):
    pieces = sems.shape[0]
    size = source.shape[0] // pieces
    return [
        pltpu.make_async_copy(
            source.at[pl.ds(i * size, size)], target.at[pl.ds(i * size, size)], sems.at[i]
        )
        for i in range(pieces)
    ]


def group_wait(source, target, sems, i):
    size = source.shape[0] // sems.shape[0]
    pltpu.make_async_copy(
        source.at[pl.ds(0, size)], target.at[pl.ds(0, size)], sems.at[i]
    ).wait()


def pack_round(step, rounds, pos, offs, tiles, packed, outs, sems, me):
    found = []
    for i, tile in enumerate(tiles):
        start = window(offs, step * GROUP + i * PAIR)
        row = jnp.concatenate([pos[i * PAIR + j : i * PAIR + j + 1, :] for j in range(PAIR)], axis=1)
        found.append((start, kept_rows(row, start, tile)))
    for start, part in found:
        put_rows(packed, start, part)
    last = step == rounds - 1

    @pl.when(last)
    def _():
        start, part = found[-1]
        clear(packed, start + part.shape[0])

    before = jnp.where(step == 0, 0, window(offs, step * GROUP))
    now = window(offs, jnp.where(last, 0, (step + 1) * GROUP))
    send_ready(packed, outs, sems, me, before, now, last)


def part_copies(packed, parts, sems, me, outward):
    count = len(parts)
    size = parts[0].shape[0]
    copies = []
    for shift, part in enumerate(parts):
        owner = lax.rem(me + (shift if outward else count - shift), count)
        where = packed.at[pl.ds(pl.multiple_of(owner * size, ALIGN), size), :]
        ends = (where, part) if outward else (part, where)
        copies.append(pltpu.make_async_copy(*ends, sems.at[shift]))
    return copies


def compact_kernel(me_ref, quality_ref, v_ref, pos_ref, offs_ref, *rest):
    outs, (tiles, packed, sems, in_sems, offs, offs_sem) = rest[:-6], rest[-6:]
    nblk, block_rows = pos_ref.shape
    rounds = nblk // GROUP
    for copy in group_copies(v_ref, tiles, in_sems):
        copy.start()
    plan(quality_ref[...], pos_ref, offs_ref)
    copy = pltpu.make_async_copy(offs_ref, offs, offs_sem)
    copy.start()
    packed[:ALIGN, :] = jnp.zeros((ALIGN, packed.shape[1]), packed.dtype)
    copy.wait()

    def body(step, carry):
        group_wait(v_ref, tiles, in_sems, step)
        pos = pos_ref[pl.ds(pl.multiple_of(step * GROUP, GROUP), GROUP), :]
        span = PAIR * block_rows
        made = []
        for i in range(GROUP // PAIR):
            at = pl.multiple_of(step * (GROUP * block_rows) + i * span, span)
            made.append(tiles[pl.ds(at, span), :])
        pack_round(step, rounds, pos, offs, made, packed, outs, sems, me_ref[0])
        return carry

    lax.fori_loop(0, rounds, body, 0)
    for copy in part_copies(packed, outs, sems, me_ref[0], True):
        copy.wait()


def part_shapes(size, count, width):
    return (jax.ShapeDtypeStruct((size, width), jnp.bfloat16),) * count


def compact(v, quality, me, size, count):
    rows, width = v.shape
    nblk, block_rows = quality.shape
    shapes = part_shapes(size, count, width)
    plan_shapes = (
        jax.ShapeDtypeStruct((nblk, block_rows), jnp.int32),
        jax.ShapeDtypeStruct((8, nblk), jnp.int32),
    )
    pos, offs, *parts = pl.pallas_call(
        compact_kernel,
        out_shape=plan_shapes + shapes,
        grid_spec=pltpu.PrefetchScalarGridSpec(
            num_scalar_prefetch=1,
            grid=(1,),
            in_specs=[
                pl.BlockSpec((nblk, block_rows), lambda i, *_: (0, 0)),
                pl.BlockSpec(memory_space=pl.ANY),
            ],
            out_specs=[
                pl.BlockSpec((nblk, block_rows), lambda i, *_: (0, 0)),
                pl.BlockSpec((8, nblk), lambda i, *_: (0, 0)),
            ]
            + [pl.BlockSpec(memory_space=pl.ANY)] * len(shapes),
            scratch_shapes=[
                pltpu.VMEM((rows, width), jnp.bfloat16),
                pltpu.VMEM((rows + ALIGN, width), jnp.bfloat16),
                pltpu.SemaphoreType.DMA((len(shapes),)),
                pltpu.SemaphoreType.DMA((nblk // GROUP,)),
                pltpu.SMEM((8, nblk), jnp.int32),
                pltpu.SemaphoreType.DMA,
            ],
        ),
        compiler_params=params(16),
        cost_estimate=pl.CostEstimate(
            flops=2 * rows * 272 * width, bytes_accessed=4 * rows * width, transcendentals=0
        ),
    )(me, quality, v)
    return pos, offs, tuple(parts)


def load_owner(packed, ins, sems, me, owner):
    count = len(ins)
    size = ins[0].shape[0]
    for shift, part in enumerate(ins):

        @pl.when(lax.rem(me + count - shift, count) == owner)
        def _():
            pltpu.make_async_copy(
                part, packed.at[pl.ds(owner * size, size), :], sems.at[owner]
            ).start()


def expand_kernel(me_ref, offs_ref, pos_ref, *rest):
    ins, (out_ref, packed, tiles, sems, out_sems) = rest[:-5], rest[-5:]
    nblk, block_rows = pos_ref.shape
    rounds = nblk // GROUP
    span = EXPAND * block_rows
    held = len(ins) * ins[0].shape[0]
    size = ins[0].shape[0]
    for piece in range(len(ins)):
        load_owner(packed, ins, sems, me_ref[0], piece)
    clear(packed, held)

    def need(step):
        end = window(offs_ref, (step + 1) * GROUP - EXPAND) + span + ALIGN
        return jnp.where(step == rounds - 1, held, jnp.minimum(end, held))

    def arrive(step):
        before = jnp.where(step == 0, 0, need(jnp.maximum(step - 1, 0)))
        now = need(step)
        for owner in range(len(ins)):

            @pl.when((owner * size >= before) & (owner * size < now))
            def _():
                pltpu.make_async_copy(
                    ins[0], packed.at[pl.ds(owner * size, size), :], sems.at[owner]
                ).wait()

    def body(step, carry):
        arrive(step)
        pos = pos_ref[pl.ds(pl.multiple_of(step * GROUP, GROUP), GROUP), :]
        made = []
        for i in range(0, GROUP, EXPAND):
            start = window(offs_ref, step * GROUP + i)
            row = jnp.concatenate([pos[i + j : i + j + 1, :] for j in range(EXPAND)], axis=1)
            at = lax.broadcasted_iota(jnp.int32, (span + ALIGN, span), 0) + start
            chosen = jnp.where(at == row, 1.0, 0.0).astype(jnp.bfloat16)
            made.append(
                lax.dot_general(
                    chosen,
                    packed[pl.ds(start, span + ALIGN), :],
                    (((0,), (0,)), ((), ())),
                    preferred_element_type=jnp.float32,
                ).astype(jnp.bfloat16)
            )
        step_rows = GROUP * block_rows
        base = pl.multiple_of(step * step_rows, step_rows)
        for i, rows in enumerate(made):
            tiles[pl.ds(pl.multiple_of(base + i * span, span), span), :] = rows
        pltpu.make_async_copy(
            tiles.at[pl.ds(base, step_rows)],
            out_ref.at[pl.ds(base, step_rows)],
            out_sems.at[step],
        ).start()
        return carry

    lax.fori_loop(0, rounds, body, 0)
    for copy in group_copies(tiles, out_ref, out_sems):
        copy.wait()


def expand(parts, pos, offs, me):
    nblk, block_rows = pos.shape
    rows = nblk * block_rows
    width = parts[0].shape[1]
    return pl.pallas_call(
        expand_kernel,
        out_shape=jax.ShapeDtypeStruct((rows, width), jnp.bfloat16),
        grid_spec=pltpu.PrefetchScalarGridSpec(
            num_scalar_prefetch=2,
            grid=(1,),
            in_specs=[pl.BlockSpec((nblk, block_rows), lambda i, *_: (0, 0))]
            + [pl.BlockSpec(memory_space=pl.ANY)] * len(parts),
            out_specs=pl.BlockSpec(memory_space=pl.ANY),
            scratch_shapes=[
                pltpu.VMEM((rows + ALIGN, width), jnp.bfloat16),
                pltpu.VMEM((rows, width), jnp.bfloat16),
                pltpu.SemaphoreType.DMA((len(parts),)),
                pltpu.SemaphoreType.DMA((nblk // GROUP,)),
            ],
        ),
        compiler_params=params(16),
        cost_estimate=pl.CostEstimate(
            flops=2 * rows * 256 * width, bytes_accessed=4 * rows * width, transcendentals=0
        ),
    )(me, offs, pos, *parts)


def spatial_kernel(
    compacting, me_ref, offs_ref, ids_ref, counts_ref, pos_ref, weight_ref, near, own, far, _, *rest
):
    nblk, block_rows = pos_ref.shape
    slots = weight_ref.shape[1]
    rounds = nblk // GROUP
    scratch = 6
    outs, (tiles, weights, halo_sems, weight_sems, made, sems) = rest[:-scratch], rest[-scratch:]
    rows = tiles.shape[0] // 3
    loads = group_copies(weight_ref, weights, weight_sems)
    loads[0].start()
    halo = [
        pltpu.make_async_copy(source, tiles.at[pl.ds(i * rows, rows), :], halo_sems.at[i])
        for i, source in enumerate((near, own, far))
    ]
    for copy in halo + loads[1:]:
        copy.start()
    if compacting:
        made[:ALIGN, :] = jnp.zeros((ALIGN, made.shape[1]), made.dtype)
    for copy in halo:
        copy.wait()

    def product(step, i):
        block = step * GROUP + i
        used = counts_ref[block]
        live = []
        picked = []
        for slot in range(slots):
            at = ids_ref[block * slots + slot]
            scale = jnp.where(slot < used, 1.0, 0.0).astype(jnp.bfloat16)
            live.append(weights[block, slot] * scale)
            start = pl.multiple_of(at * block_rows, block_rows)
            picked.append(tiles[pl.ds(start, block_rows), :])
        return jnp.dot(
            jnp.concatenate(live, axis=1),
            jnp.concatenate(picked, axis=0),
            preferred_element_type=jnp.float32,
        ).astype(jnp.bfloat16)

    def body(step, carry):
        group_wait(weight_ref, weights, weight_sems, step)
        pos = pos_ref[pl.ds(pl.multiple_of(step * GROUP, GROUP), GROUP), :]
        found = [product(step, i) for i in range(GROUP)]
        if compacting:
            found = [
                jnp.concatenate(found[i : i + PAIR], axis=0) for i in range(0, GROUP, PAIR)
            ]
            pack_round(step, rounds, pos, offs_ref, found, made, outs, sems, me_ref[0])
            return carry
        a = lax.broadcasted_iota(jnp.int32, (block_rows, block_rows), 0)
        b = lax.broadcasted_iota(jnp.int32, (block_rows, block_rows), 1)
        size = GROUP * block_rows
        base = pl.multiple_of(step * size, size)
        for i in range(GROUP):
            kept = jnp.where((a == b) & (pos[i : i + 1, :] >= 0), 1.0, 0.0).astype(jnp.bfloat16)
            made[pl.ds(pl.multiple_of(base + i * block_rows, block_rows), block_rows), :] = jnp.dot(
                kept, found[i], preferred_element_type=jnp.float32
            ).astype(jnp.bfloat16)
        pltpu.make_async_copy(
            made.at[pl.ds(base, size)], outs[0].at[pl.ds(base, size)], sems.at[step]
        ).start()
        return carry

    lax.fori_loop(0, rounds, body, 0)
    if compacting:
        copies = part_copies(made, outs, sems, me_ref[0], True)
    else:
        copies = group_copies(made, outs[0], sems)
    for copy in copies:
        copy.wait()


def spatial(halo, weights, ids, counts, pos, offs, me, size, count):
    rows, width = halo[1].shape
    nblk, block_rows = pos.shape
    slots = weights.shape[1]
    any_spec = pl.BlockSpec(memory_space=pl.ANY)
    rounds = nblk // GROUP
    if size is None:
        shapes = (jax.ShapeDtypeStruct((rows, width), jnp.bfloat16),)
        made = (rows, rounds)
    else:
        shapes = part_shapes(size, count, width)
        made = (rows + ALIGN, len(shapes))
    return pl.pallas_call(
        functools.partial(spatial_kernel, size is not None),
        out_shape=shapes,
        grid_spec=pltpu.PrefetchScalarGridSpec(
            num_scalar_prefetch=4,
            grid=(1,),
            in_specs=[pl.BlockSpec((nblk, block_rows), lambda i, *_: (0, 0))] + [any_spec] * 5,
            out_specs=[any_spec] * len(shapes),
            scratch_shapes=[
                pltpu.VMEM((3 * rows, width), jnp.bfloat16),
                pltpu.VMEM(weights.shape, jnp.bfloat16),
                pltpu.SemaphoreType.DMA((3,)),
                pltpu.SemaphoreType.DMA((rounds,)),
                pltpu.VMEM((made[0], width), jnp.bfloat16),
                pltpu.SemaphoreType.DMA((made[1],)),
            ],
        ),
        compiler_params=params(34),
        cost_estimate=pl.CostEstimate(
            flops=2 * rows * slots * block_rows * width,
            bytes_accessed=8 * rows * width + 2 * rows * slots * block_rows,
            transcendentals=0,
        ),
    )(me, offs, ids, counts, pos, weights, *halo)


def mix_kernel(count, me_ref, op_ref, *rest):
    ins, outs, (rolled, sems) = rest[:count], rest[count : 2 * count], rest[2 * count :]
    width = ins[0].shape[1]
    me = me_ref[0]

    @pl.when(pl.program_id(0) == 0)
    def _():
        copies = []
        for shift in range(count):
            source = lax.rem(me + count - shift, count)
            copies.append(
                pltpu.make_async_copy(
                    op_ref.at[pl.ds(pl.multiple_of(source * width, ALIGN), width), :],
                    rolled.at[pl.ds(shift * width, width), :],
                    sems.at[shift],
                )
            )
        for copy in copies:
            copy.start()
        for copy in copies:
            copy.wait()

    row = jnp.concatenate([part[...] for part in ins], axis=1)
    for shift in range(count):
        dest = lax.rem(me + shift, count)
        columns = rolled[:, pl.ds(pl.multiple_of(dest * width, 128), width)]
        outs[shift][...] = jnp.dot(row, columns, preferred_element_type=jnp.float32).astype(
            jnp.bfloat16
        )


def mix(parts, chan_op, me):
    count = len(parts)
    rows, width = parts[0].shape
    tiles = [t for t in range(ALIGN, min(rows, 640) + 1, ALIGN) if rows % t == 0]
    tile = tiles[-1]
    spec = pl.BlockSpec((tile, width), lambda i, *_: (i, 0))
    return pl.pallas_call(
        functools.partial(mix_kernel, count),
        out_shape=part_shapes(rows, count, width),
        grid_spec=pltpu.PrefetchScalarGridSpec(
            num_scalar_prefetch=1,
            grid=(rows // tile,),
            in_specs=[pl.BlockSpec(memory_space=pl.ANY)] + [spec] * count,
            out_specs=[spec] * count,
            scratch_shapes=[
                pltpu.VMEM(chan_op.shape, jnp.bfloat16),
                pltpu.SemaphoreType.DMA((count,)),
            ],
        ),
        compiler_params=params(16),
        cost_estimate=pl.CostEstimate(flops=1, bytes_accessed=1, transcendentals=0),
    )(me, chan_op, *parts)


class Line:
    def __init__(self, depth):
        self.depth = depth
        self.done = []

    def exchange(self, parts):
        count = len(parts)
        arrived = list(parts)
        for shift in sorted(range(1, count), key=lambda k: min(k, count - k)):
            part = parts[shift]
            if len(self.done) >= self.depth:
                part = after(part, self.done[-self.depth])
            arrived[shift] = lax.ppermute(
                part, "chan", [(i, (i + shift) % count) for i in range(count)]
            )
            self.done.append(arrived[shift])
        return tuple(arrived)


def after(values, *others):
    return lax.optimization_barrier((values, others))[0]


def gate_kernel(x_ref, out_ref):
    out_ref[...] = x_ref[...]


def gate(x):
    shape = (ALIGN, x.shape[1])
    spec = pl.BlockSpec(shape, lambda i: (0, 0))
    return pl.pallas_call(
        gate_kernel,
        out_shape=jax.ShapeDtypeStruct(shape, x.dtype),
        grid=(1,),
        in_specs=[spec],
        out_specs=spec,
        cost_estimate=pl.CostEstimate(flops=10**11, bytes_accessed=1, transcendentals=0),
    )(x)


def halo_of(x):
    count = lax.axis_size("orbit")
    far = [(i, i + 1) for i in range(1, count - 1, 2)]
    far = lax.ppermute(x, "orbit", far + [(b, a) for a, b in far])
    near = [(i, i + 1) for i in range(0, count - 1, 2)]
    near = lax.ppermute(x, "orbit", near + [(b, a) for a, b in near])
    return near, x, far


def halo_ids(neighbours, nblk):
    mine = lax.axis_index("orbit")
    local = jnp.clip(neighbours - (mine - 1) * nblk, 0, 3 * nblk - 1)
    side = local // nblk
    side = jnp.where(mine % 2 == 0, 2 - side, side)
    return (side * nblk + local % nblk).reshape(-1)


def weigh(
    innovation, perturbation, quality, neighbours, counts, spatial_blocks, chan_op, capacity, watch
):
    rows, width = innovation.shape
    block_rows = spatial_blocks.shape[2]
    nblk = rows // block_rows
    count = lax.axis_size("chan")
    size = capacity // count

    me = lax.axis_index("chan").astype(jnp.int32).reshape(1)
    ids = halo_ids(neighbours, nblk)

    def spread(halo, room):
        return spatial(halo, spatial_blocks, ids, counts, pos, offs, me, room, count)

    kept = quality.reshape(nblk, block_rows)
    pos, offs, parts_i = compact(innovation, kept, me, size, count)
    line = Line(DEPTH)
    there_i = line.exchange(parts_i)
    perturbation, quality = after((perturbation, quality), parts_i[0])
    masked_p = perturbation * quality.astype(jnp.bfloat16)[:, None]
    parts_p = spread((*halo_of(masked_p), gate(there_i[1 % count])), size)
    there_p = line.exchange(parts_p)

    mixed_i = mix(after(there_i, parts_p[0]), chan_op, me)
    back_i = line.exchange(mixed_i)
    seen = watch(after(quality, parts_p[0]))
    mixed_p = mix(after(there_p, (mixed_i[0], seen)), chan_op, me)
    back_p = line.exchange(after(mixed_p, back_i))

    wide_i = expand(after(back_i, mixed_p[0]), pos, offs, me)
    (out_i,) = spread((*halo_of(wide_i), gate(back_p[count // 2])), None)
    out_p = expand(after(back_p, out_i), pos, offs, me)
    return (out_i, out_p), seen


def shards(innovation, perturbation, quality, *others):
    rows = innovation.shape[0]
    unit = ALIGN * lax.axis_size("chan")
    capacity = -(-rows * 57 // (64 * unit)) * unit
    given = (innovation, perturbation, quality, *others)

    def overfull(quality):
        more = jnp.sum(quality, dtype=jnp.int32) > capacity
        return lax.pmax(more.astype(jnp.int32), ("grp", "orbit"))

    packed, more = weigh(*given, capacity, overfull)
    return lax.cond(
        more > 0,
        lambda given, packed: weigh(*given, rows, lambda quality: None)[0],
        lambda given, packed: packed,
        given,
        packed,
    )


def solution(mesh):
    placed = (
        P(("grp", "orbit"), "chan"),
        P(("grp", "orbit"), "chan"),
        P(("grp", "orbit")),
        P(("grp", "orbit"), None),
        P(("grp", "orbit")),
        P(("grp", "orbit"), None, None, None),
        P(),
    )
    return jax.shard_map(
        shards,
        mesh=mesh,
        in_specs=placed,
        out_specs=(P(("grp", "orbit"), "chan"), P(("grp", "orbit"), "chan")),
        check_vma=False,
    )
```

```python
import functools

import jax
import jax.numpy as jnp
from jax import lax
from jax.experimental import pallas as pl
from jax.experimental.pallas import tpu as pltpu
from jax.sharding import PartitionSpec as P

MIB = 1024 * 1024
ALIGN = 16
DEPTH = 4
PAIR = 2
EXPAND = 1
GROUP = 16


def params(mib):
    return pltpu.CompilerParams(
        dimension_semantics=("arbitrary",), vmem_limit_bytes=mib * MIB
    )


def plan(quality, pos_ref, offs_ref):
    blocks, rows = quality.shape
    ones = quality.astype(jnp.float32).astype(jnp.bfloat16)

    def ahead(size):
        a = lax.broadcasted_iota(jnp.int32, (size, size), 0)
        b = lax.broadcasted_iota(jnp.int32, (size, size), 1)
        return jnp.where(a < b, 1.0, 0.0).astype(jnp.bfloat16)

    def dot(a, b, dims=((1,), (0,))):
        return lax.dot_general(a, b, (dims, ((), ())), preferred_element_type=jnp.float32)

    within = dot(ones, ahead(rows))
    totals = dot(jnp.ones((8, rows), jnp.bfloat16), ones, ((1,), (1,)))
    first = dot(totals.astype(jnp.bfloat16), ahead(blocks))
    offs_ref[...] = first.astype(jnp.int32)
    wide = jnp.broadcast_to(jnp.sum(ones.astype(jnp.float32), axis=1, keepdims=True), (blocks, rows))
    before = dot(ahead(blocks), wide.astype(jnp.bfloat16), ((0,), (0,)))
    pos_ref[...] = jnp.where(quality > 0, (before + within).astype(jnp.int32), -1)


def window(offs_ref, block):
    return pl.multiple_of((offs_ref[0, block] // ALIGN) * ALIGN, ALIGN)


def kept_rows(pos, start, tile):
    rows = tile.shape[0]
    at = lax.broadcasted_iota(jnp.int32, (rows + ALIGN, rows), 0) + start
    chosen = jnp.where(at == pos, 1.0, 0.0).astype(jnp.bfloat16)
    return jnp.dot(chosen, tile, preferred_element_type=jnp.float32).astype(jnp.bfloat16)


def put_rows(packed, start, part):
    rest = part.shape[0] - ALIGN
    packed[pl.ds(start, ALIGN), :] = packed[pl.ds(start, ALIGN), :] + part[:ALIGN]
    packed[pl.ds(pl.multiple_of(start + ALIGN, ALIGN), rest), :] = part[ALIGN:]


def clear(ref, start):
    def body(i, carry):
        at = pl.multiple_of(i * ALIGN, ALIGN)
        ref[pl.ds(at, ALIGN), :] = jnp.zeros((ALIGN, ref.shape[1]), ref.dtype)
        return carry

    lax.fori_loop(start // ALIGN, ref.shape[0] // ALIGN, body, 0)


def send_ready(packed, outs, sems, me, before, now, last):
    count = len(outs)
    size = outs[0].shape[0]
    for shift, copy in enumerate(part_copies(packed, outs, sems, me, True)):
        past = (lax.rem(me + shift, count) + 1) * size

        @pl.when((past > before) & ((past <= now) | last))
        def _():
            copy.start()


def group_copies(source, target, sems):
    pieces = sems.shape[0]
    size = source.shape[0] // pieces
    return [
        pltpu.make_async_copy(
            source.at[pl.ds(i * size, size)], target.at[pl.ds(i * size, size)], sems.at[i]
        )
        for i in range(pieces)
    ]


def group_wait(source, target, sems, i):
    size = source.shape[0] // sems.shape[0]
    pltpu.make_async_copy(
        source.at[pl.ds(0, size)], target.at[pl.ds(0, size)], sems.at[i]
    ).wait()


def pack_round(step, rounds, pos, offs, tiles, packed, outs, sems, me):
    found = []
    for i, tile in enumerate(tiles):
        start = window(offs, step * GROUP + i * PAIR)
        row = jnp.concatenate([pos[i * PAIR + j : i * PAIR + j + 1, :] for j in range(PAIR)], axis=1)
        found.append((start, kept_rows(row, start, tile)))
    for start, part in found:
        put_rows(packed, start, part)
    last = step == rounds - 1

    @pl.when(last)
    def _():
        start, part = found[-1]
        clear(packed, start + part.shape[0])

    before = jnp.where(step == 0, 0, window(offs, step * GROUP))
    now = window(offs, jnp.where(last, 0, (step + 1) * GROUP))
    send_ready(packed, outs, sems, me, before, now, last)


def part_copies(packed, parts, sems, me, outward):
    count = len(parts)
    size = parts[0].shape[0]
    copies = []
    for shift, part in enumerate(parts):
        owner = lax.rem(me + (shift if outward else count - shift), count)
        where = packed.at[pl.ds(pl.multiple_of(owner * size, ALIGN), size), :]
        ends = (where, part) if outward else (part, where)
        copies.append(pltpu.make_async_copy(*ends, sems.at[shift]))
    return copies


def compact_kernel(me_ref, quality_ref, v_ref, pos_ref, offs_ref, *rest):
    outs, (tiles, packed, sems, in_sems, offs, offs_sem) = rest[:-6], rest[-6:]
    nblk, block_rows = pos_ref.shape
    rounds = nblk // GROUP
    for copy in group_copies(v_ref, tiles, in_sems):
        copy.start()
    plan(quality_ref[...], pos_ref, offs_ref)
    copy = pltpu.make_async_copy(offs_ref, offs, offs_sem)
    copy.start()
    packed[:ALIGN, :] = jnp.zeros((ALIGN, packed.shape[1]), packed.dtype)
    copy.wait()

    def body(step, carry):
        group_wait(v_ref, tiles, in_sems, step)
        pos = pos_ref[pl.ds(pl.multiple_of(step * GROUP, GROUP), GROUP), :]
        span = PAIR * block_rows
        made = []
        for i in range(GROUP // PAIR):
            at = pl.multiple_of(step * (GROUP * block_rows) + i * span, span)
            made.append(tiles[pl.ds(at, span), :])
        pack_round(step, rounds, pos, offs, made, packed, outs, sems, me_ref[0])
        return carry

    lax.fori_loop(0, rounds, body, 0)
    for copy in part_copies(packed, outs, sems, me_ref[0], True):
        copy.wait()


def part_shapes(size, count, width):
    return (jax.ShapeDtypeStruct((size, width), jnp.bfloat16),) * count


def compact(v, quality, me, size, count):
    rows, width = v.shape
    nblk, block_rows = quality.shape
    shapes = part_shapes(size, count, width)
    plan_shapes = (
        jax.ShapeDtypeStruct((nblk, block_rows), jnp.int32),
        jax.ShapeDtypeStruct((8, nblk), jnp.int32),
    )
    pos, offs, *parts = pl.pallas_call(
        compact_kernel,
        out_shape=plan_shapes + shapes,
        grid_spec=pltpu.PrefetchScalarGridSpec(
            num_scalar_prefetch=1,
            grid=(1,),
            in_specs=[
                pl.BlockSpec((nblk, block_rows), lambda i, *_: (0, 0)),
                pl.BlockSpec(memory_space=pl.ANY),
            ],
            out_specs=[
                pl.BlockSpec((nblk, block_rows), lambda i, *_: (0, 0)),
                pl.BlockSpec((8, nblk), lambda i, *_: (0, 0)),
            ]
            + [pl.BlockSpec(memory_space=pl.ANY)] * len(shapes),
            scratch_shapes=[
                pltpu.VMEM((rows, width), jnp.bfloat16),
                pltpu.VMEM((rows + ALIGN, width), jnp.bfloat16),
                pltpu.SemaphoreType.DMA((len(shapes),)),
                pltpu.SemaphoreType.DMA((nblk // GROUP,)),
                pltpu.SMEM((8, nblk), jnp.int32),
                pltpu.SemaphoreType.DMA,
            ],
        ),
        compiler_params=params(16),
        cost_estimate=pl.CostEstimate(
            flops=2 * rows * 272 * width, bytes_accessed=4 * rows * width, transcendentals=0
        ),
    )(me, quality, v)
    return pos, offs, tuple(parts)


def load_owner(packed, ins, sems, me, owner):
    count = len(ins)
    size = ins[0].shape[0]
    for shift, part in enumerate(ins):

        @pl.when(lax.rem(me + count - shift, count) == owner)
        def _():
            pltpu.make_async_copy(
                part, packed.at[pl.ds(owner * size, size), :], sems.at[owner]
            ).start()


def expand_kernel(me_ref, offs_ref, pos_ref, *rest):
    ins, (out_ref, packed, tiles, sems, out_sems) = rest[:-5], rest[-5:]
    nblk, block_rows = pos_ref.shape
    rounds = nblk // GROUP
    span = EXPAND * block_rows
    held = len(ins) * ins[0].shape[0]
    size = ins[0].shape[0]
    for piece in range(len(ins)):
        load_owner(packed, ins, sems, me_ref[0], piece)
    clear(packed, held)

    def need(step):
        end = window(offs_ref, (step + 1) * GROUP - EXPAND) + span + ALIGN
        return jnp.where(step == rounds - 1, held, jnp.minimum(end, held))

    def arrive(step):
        before = jnp.where(step == 0, 0, need(jnp.maximum(step - 1, 0)))
        now = need(step)
        for owner in range(len(ins)):

            @pl.when((owner * size >= before) & (owner * size < now))
            def _():
                pltpu.make_async_copy(
                    ins[0], packed.at[pl.ds(owner * size, size), :], sems.at[owner]
                ).wait()

    def body(step, carry):
        arrive(step)
        pos = pos_ref[pl.ds(pl.multiple_of(step * GROUP, GROUP), GROUP), :]
        made = []
        for i in range(0, GROUP, EXPAND):
            start = window(offs_ref, step * GROUP + i)
            row = jnp.concatenate([pos[i + j : i + j + 1, :] for j in range(EXPAND)], axis=1)
            at = lax.broadcasted_iota(jnp.int32, (span + ALIGN, span), 0) + start
            chosen = jnp.where(at == row, 1.0, 0.0).astype(jnp.bfloat16)
            made.append(
                lax.dot_general(
                    chosen,
                    packed[pl.ds(start, span + ALIGN), :],
                    (((0,), (0,)), ((), ())),
                    preferred_element_type=jnp.float32,
                ).astype(jnp.bfloat16)
            )
        step_rows = GROUP * block_rows
        base = pl.multiple_of(step * step_rows, step_rows)
        for i, rows in enumerate(made):
            tiles[pl.ds(pl.multiple_of(base + i * span, span), span), :] = rows
        pltpu.make_async_copy(
            tiles.at[pl.ds(base, step_rows)],
            out_ref.at[pl.ds(base, step_rows)],
            out_sems.at[step],
        ).start()
        return carry

    lax.fori_loop(0, rounds, body, 0)
    for copy in group_copies(tiles, out_ref, out_sems):
        copy.wait()


def expand(parts, pos, offs, me):
    nblk, block_rows = pos.shape
    rows = nblk * block_rows
    width = parts[0].shape[1]
    return pl.pallas_call(
        expand_kernel,
        out_shape=jax.ShapeDtypeStruct((rows, width), jnp.bfloat16),
        grid_spec=pltpu.PrefetchScalarGridSpec(
            num_scalar_prefetch=2,
            grid=(1,),
            in_specs=[pl.BlockSpec((nblk, block_rows), lambda i, *_: (0, 0))]
            + [pl.BlockSpec(memory_space=pl.ANY)] * len(parts),
            out_specs=pl.BlockSpec(memory_space=pl.ANY),
            scratch_shapes=[
                pltpu.VMEM((rows + ALIGN, width), jnp.bfloat16),
                pltpu.VMEM((rows, width), jnp.bfloat16),
                pltpu.SemaphoreType.DMA((len(parts),)),
                pltpu.SemaphoreType.DMA((nblk // GROUP,)),
            ],
        ),
        compiler_params=params(16),
        cost_estimate=pl.CostEstimate(
            flops=2 * rows * 256 * width, bytes_accessed=4 * rows * width, transcendentals=0
        ),
    )(me, offs, pos, *parts)


def rounds_of(nblk, compacting):
    return nblk // GROUP if compacting else max(nblk // (2 * GROUP), 1)


def spatial_kernel(
    compacting, me_ref, offs_ref, ids_ref, counts_ref, pos_ref, weight_ref, near, own, far, _, *rest
):
    nblk, block_rows = pos_ref.shape
    slots = weight_ref.shape[1]
    rounds = rounds_of(nblk, compacting)
    group = nblk // rounds
    scratch = 6
    outs, (tiles, weights, halo_sems, weight_sems, made, sems) = rest[:-scratch], rest[-scratch:]
    rows = tiles.shape[0] // 3
    loads = group_copies(weight_ref, weights, weight_sems)
    loads[0].start()
    halo = [
        pltpu.make_async_copy(source, tiles.at[pl.ds(i * rows, rows), :], halo_sems.at[i])
        for i, source in enumerate((near, own, far))
    ]
    for copy in halo + loads[1:]:
        copy.start()
    if compacting:
        made[:ALIGN, :] = jnp.zeros((ALIGN, made.shape[1]), made.dtype)
    for copy in halo:
        copy.wait()

    def product(step, i):
        block = step * group + i
        used = counts_ref[block]
        live = []
        picked = []
        for slot in range(slots):
            at = ids_ref[block * slots + slot]
            scale = jnp.where(slot < used, 1.0, 0.0).astype(jnp.bfloat16)
            live.append(weights[block, slot] * scale)
            start = pl.multiple_of(at * block_rows, block_rows)
            picked.append(tiles[pl.ds(start, block_rows), :])
        return jnp.dot(
            jnp.concatenate(live, axis=1),
            jnp.concatenate(picked, axis=0),
            preferred_element_type=jnp.float32,
        ).astype(jnp.bfloat16)

    def body(step, carry):
        group_wait(weight_ref, weights, weight_sems, step)
        pos = pos_ref[pl.ds(pl.multiple_of(step * group, group), group), :]
        found = [product(step, i) for i in range(group)]
        if compacting:
            found = [
                jnp.concatenate(found[i : i + PAIR], axis=0) for i in range(0, group, PAIR)
            ]
            pack_round(step, rounds, pos, offs_ref, found, made, outs, sems, me_ref[0])
            return carry
        size = group * block_rows
        base = pl.multiple_of(step * size, size)
        for i in range(group):
            kept = jnp.where(pos[i : i + 1, :] >= 0, 1.0, 0.0)
            kept = jnp.broadcast_to(kept, (block_rows, block_rows)).T.astype(jnp.bfloat16)
            kept = jnp.concatenate([kept] * (made.shape[1] // block_rows), axis=1)
            made[pl.ds(pl.multiple_of(base + i * block_rows, block_rows), block_rows), :] = (
                found[i] * kept
            )
        pltpu.make_async_copy(
            made.at[pl.ds(base, size)], outs[0].at[pl.ds(base, size)], sems.at[step]
        ).start()
        return carry

    lax.fori_loop(0, rounds, body, 0)
    if compacting:
        copies = part_copies(made, outs, sems, me_ref[0], True)
    else:
        copies = group_copies(made, outs[0], sems)
    for copy in copies:
        copy.wait()


def spatial(halo, weights, ids, counts, pos, offs, me, size, count):
    rows, width = halo[1].shape
    nblk, block_rows = pos.shape
    slots = weights.shape[1]
    any_spec = pl.BlockSpec(memory_space=pl.ANY)
    rounds = rounds_of(nblk, size is not None)
    if size is None:
        shapes = (jax.ShapeDtypeStruct((rows, width), jnp.bfloat16),)
        made = (rows, rounds)
    else:
        shapes = part_shapes(size, count, width)
        made = (rows + ALIGN, len(shapes))
    return pl.pallas_call(
        functools.partial(spatial_kernel, size is not None),
        out_shape=shapes,
        grid_spec=pltpu.PrefetchScalarGridSpec(
            num_scalar_prefetch=4,
            grid=(1,),
            in_specs=[pl.BlockSpec((nblk, block_rows), lambda i, *_: (0, 0))] + [any_spec] * 5,
            out_specs=[any_spec] * len(shapes),
            scratch_shapes=[
                pltpu.VMEM((3 * rows, width), jnp.bfloat16),
                pltpu.VMEM(weights.shape, jnp.bfloat16),
                pltpu.SemaphoreType.DMA((3,)),
                pltpu.SemaphoreType.DMA((rounds,)),
                pltpu.VMEM((made[0], width), jnp.bfloat16),
                pltpu.SemaphoreType.DMA((made[1],)),
            ],
        ),
        compiler_params=params(34),
        cost_estimate=pl.CostEstimate(
            flops=2 * rows * slots * block_rows * width,
            bytes_accessed=8 * rows * width + 2 * rows * slots * block_rows,
            transcendentals=0,
        ),
    )(me, offs, ids, counts, pos, weights, *halo)


def mix_kernel(count, me_ref, op_ref, *rest):
    ins, outs, (rolled, sems) = rest[:count], rest[count : 2 * count], rest[2 * count :]
    width = ins[0].shape[1]
    me = me_ref[0]

    @pl.when(pl.program_id(0) == 0)
    def _():
        copies = []
        for shift in range(count):
            source = lax.rem(me + count - shift, count)
            copies.append(
                pltpu.make_async_copy(
                    op_ref.at[pl.ds(pl.multiple_of(source * width, ALIGN), width), :],
                    rolled.at[pl.ds(shift * width, width), :],
                    sems.at[shift],
                )
            )
        for copy in copies:
            copy.start()
        for copy in copies:
            copy.wait()

    row = jnp.concatenate([part[...] for part in ins], axis=1)
    for shift in range(count):
        dest = lax.rem(me + shift, count)
        columns = rolled[:, pl.ds(pl.multiple_of(dest * width, 128), width)]
        outs[shift][...] = jnp.dot(row, columns, preferred_element_type=jnp.float32).astype(
            jnp.bfloat16
        )


def mix(parts, chan_op, me):
    count = len(parts)
    rows, width = parts[0].shape
    tiles = [t for t in range(ALIGN, min(rows, 640) + 1, ALIGN) if rows % t == 0]
    tile = tiles[-1]
    spec = pl.BlockSpec((tile, width), lambda i, *_: (i, 0))
    return pl.pallas_call(
        functools.partial(mix_kernel, count),
        out_shape=part_shapes(rows, count, width),
        grid_spec=pltpu.PrefetchScalarGridSpec(
            num_scalar_prefetch=1,
            grid=(rows // tile,),
            in_specs=[pl.BlockSpec(memory_space=pl.ANY)] + [spec] * count,
            out_specs=[spec] * count,
            scratch_shapes=[
                pltpu.VMEM(chan_op.shape, jnp.bfloat16),
                pltpu.SemaphoreType.DMA((count,)),
            ],
        ),
        compiler_params=params(16),
        cost_estimate=pl.CostEstimate(flops=1, bytes_accessed=1, transcendentals=0),
    )(me, chan_op, *parts)


class Line:
    def __init__(self, depth):
        self.depth = depth
        self.done = []

    def exchange(self, parts):
        count = len(parts)
        arrived = list(parts)
        for shift in sorted(range(1, count), key=lambda k: min(k, count - k)):
            part = parts[shift]
            if len(self.done) >= self.depth:
                part = after(part, self.done[-self.depth])
            arrived[shift] = lax.ppermute(
                part, "chan", [(i, (i + shift) % count) for i in range(count)]
            )
            self.done.append(arrived[shift])
        return tuple(arrived)


def after(values, *others):
    return lax.optimization_barrier((values, others))[0]


def gate_kernel(x_ref, out_ref):
    out_ref[...] = x_ref[...]


def gate(x):
    shape = (ALIGN, x.shape[1])
    spec = pl.BlockSpec(shape, lambda i: (0, 0))
    return pl.pallas_call(
        gate_kernel,
        out_shape=jax.ShapeDtypeStruct(shape, x.dtype),
        grid=(1,),
        in_specs=[spec],
        out_specs=spec,
        cost_estimate=pl.CostEstimate(flops=10**11, bytes_accessed=1, transcendentals=0),
    )(x)


def halo_of(x):
    count = lax.axis_size("orbit")
    far = [(i, i + 1) for i in range(1, count - 1, 2)]
    far = lax.ppermute(x, "orbit", far + [(b, a) for a, b in far])
    near = [(i, i + 1) for i in range(0, count - 1, 2)]
    near = lax.ppermute(x, "orbit", near + [(b, a) for a, b in near])
    return near, x, far


def halo_ids(neighbours, nblk):
    mine = lax.axis_index("orbit")
    local = jnp.clip(neighbours - (mine - 1) * nblk, 0, 3 * nblk - 1)
    side = local // nblk
    side = jnp.where(mine % 2 == 0, 2 - side, side)
    return (side * nblk + local % nblk).reshape(-1)


def weigh(
    innovation, perturbation, quality, neighbours, counts, spatial_blocks, chan_op, capacity, watch
):
    rows, width = innovation.shape
    block_rows = spatial_blocks.shape[2]
    nblk = rows // block_rows
    count = lax.axis_size("chan")
    size = capacity // count

    me = lax.axis_index("chan").astype(jnp.int32).reshape(1)
    ids = halo_ids(neighbours, nblk)

    def spread(halo, room):
        return spatial(halo, spatial_blocks, ids, counts, pos, offs, me, room, count)

    kept = quality.reshape(nblk, block_rows)
    pos, offs, parts_i = compact(innovation, kept, me, size, count)
    line = Line(DEPTH)
    there_i = line.exchange(parts_i)
    perturbation, quality = after((perturbation, quality), parts_i[0])
    masked_p = perturbation * quality.astype(jnp.bfloat16)[:, None]
    parts_p = spread((*halo_of(masked_p), gate(there_i[1 % count])), size)
    there_p = line.exchange(parts_p)

    mixed_i = mix(after(there_i, parts_p[0]), chan_op, me)
    back_i = line.exchange(mixed_i)
    seen = watch(after(quality, parts_p[0]))
    mixed_p = mix(after(there_p, (mixed_i[0], seen)), chan_op, me)
    back_p = line.exchange(after(mixed_p, back_i))

    wide_i = expand(after(back_i, mixed_p[0]), pos, offs, me)
    (out_i,) = spread((*halo_of(wide_i), gate(back_p[count // 2])), None)
    out_p = expand(after(back_p, out_i), pos, offs, me)
    return (out_i, out_p), seen


def shards(innovation, perturbation, quality, *others):
    rows = innovation.shape[0]
    unit = ALIGN * lax.axis_size("chan")
    capacity = -(-rows * 57 // (64 * unit)) * unit
    given = (innovation, perturbation, quality, *others)

    def overfull(quality):
        more = jnp.sum(quality, dtype=jnp.int32) > capacity
        return lax.pmax(more.astype(jnp.int32), ("grp", "orbit"))

    packed, more = weigh(*given, capacity, overfull)
    return lax.cond(
        more > 0,
        lambda given, packed: weigh(*given, rows, lambda quality: None)[0],
        lambda given, packed: packed,
        given,
        packed,
    )


def solution(mesh):
    placed = (
        P(("grp", "orbit"), "chan"),
        P(("grp", "orbit"), "chan"),
        P(("grp", "orbit")),
        P(("grp", "orbit"), None),
        P(("grp", "orbit")),
        P(("grp", "orbit"), None, None, None),
        P(),
    )
    return jax.shard_map(
        shards,
        mesh=mesh,
        in_specs=placed,
        out_specs=(P(("grp", "orbit"), "chan"), P(("grp", "orbit"), "chan")),
        check_vma=False,
    )
```

```python
import functools

import jax
import jax.numpy as jnp
from jax import lax
from jax.experimental import pallas as pl
from jax.experimental.pallas import tpu as pltpu
from jax.sharding import PartitionSpec as P

MIB = 1024 * 1024
ALIGN = 16
DEPTH = 4
PAIR = 2
EXPAND = 1
GROUP = 16


def params(mib):
    return pltpu.CompilerParams(
        dimension_semantics=("arbitrary",), vmem_limit_bytes=mib * MIB
    )


def plan(quality, pos_ref, offs_ref, started):
    blocks, rows = quality.shape
    ones = quality.astype(jnp.float32).astype(jnp.bfloat16)

    def ahead(size):
        a = lax.broadcasted_iota(jnp.int32, (size, size), 0)
        b = lax.broadcasted_iota(jnp.int32, (size, size), 1)
        return jnp.where(a < b, 1.0, 0.0).astype(jnp.bfloat16)

    def dot(a, b, dims=((1,), (0,))):
        return lax.dot_general(a, b, (dims, ((), ())), preferred_element_type=jnp.float32)

    totals = dot(jnp.ones((8, rows), jnp.bfloat16), ones, ((1,), (1,)))
    first = dot(totals.astype(jnp.bfloat16), ahead(blocks))
    offs_ref[...] = first.astype(jnp.int32)
    started()
    within = dot(ones, ahead(rows))
    wide = jnp.broadcast_to(jnp.sum(ones.astype(jnp.float32), axis=1, keepdims=True), (blocks, rows))
    before = dot(ahead(blocks), wide.astype(jnp.bfloat16), ((0,), (0,)))
    pos_ref[...] = jnp.where(quality > 0, (before + within).astype(jnp.int32), -1)


def window(offs_ref, block):
    return pl.multiple_of((offs_ref[0, block] // ALIGN) * ALIGN, ALIGN)


def kept_rows(pos, start, tile):
    rows = tile.shape[0]
    at = lax.broadcasted_iota(jnp.int32, (rows + ALIGN, rows), 0) + start
    chosen = jnp.where(at == pos, 1.0, 0.0).astype(jnp.bfloat16)
    return jnp.dot(chosen, tile, preferred_element_type=jnp.float32).astype(jnp.bfloat16)


def put_rows(packed, start, part):
    rest = part.shape[0] - ALIGN
    packed[pl.ds(start, ALIGN), :] = packed[pl.ds(start, ALIGN), :] + part[:ALIGN]
    packed[pl.ds(pl.multiple_of(start + ALIGN, ALIGN), rest), :] = part[ALIGN:]


def clear(ref, start):
    def body(i, carry):
        at = pl.multiple_of(i * ALIGN, ALIGN)
        ref[pl.ds(at, ALIGN), :] = jnp.zeros((ALIGN, ref.shape[1]), ref.dtype)
        return carry

    lax.fori_loop(start // ALIGN, ref.shape[0] // ALIGN, body, 0)


def send_ready(packed, outs, sems, me, before, now, last):
    count = len(outs)
    size = outs[0].shape[0]
    for shift, copy in enumerate(part_copies(packed, outs, sems, me, True)):
        past = (lax.rem(me + shift, count) + 1) * size

        @pl.when((past > before) & ((past <= now) | last))
        def _():
            copy.start()


def group_copies(source, target, sems):
    pieces = sems.shape[0]
    size = source.shape[0] // pieces
    return [
        pltpu.make_async_copy(
            source.at[pl.ds(i * size, size)], target.at[pl.ds(i * size, size)], sems.at[i]
        )
        for i in range(pieces)
    ]


def group_wait(source, target, sems, i):
    size = source.shape[0] // sems.shape[0]
    pltpu.make_async_copy(
        source.at[pl.ds(0, size)], target.at[pl.ds(0, size)], sems.at[i]
    ).wait()


def pack_round(step, rounds, pos, offs, tiles, packed, outs, sems, me):
    found = []
    for i, tile in enumerate(tiles):
        start = window(offs, step * GROUP + i * PAIR)
        row = jnp.concatenate([pos[i * PAIR + j : i * PAIR + j + 1, :] for j in range(PAIR)], axis=1)
        found.append((start, kept_rows(row, start, tile)))
    for start, part in found:
        put_rows(packed, start, part)
    last = step == rounds - 1

    @pl.when(last)
    def _():
        start, part = found[-1]
        clear(packed, start + part.shape[0])

    before = jnp.where(step == 0, 0, window(offs, step * GROUP))
    now = window(offs, jnp.where(last, 0, (step + 1) * GROUP))
    send_ready(packed, outs, sems, me, before, now, last)


def part_copies(packed, parts, sems, me, outward):
    count = len(parts)
    size = parts[0].shape[0]
    copies = []
    for shift, part in enumerate(parts):
        owner = lax.rem(me + (shift if outward else count - shift), count)
        where = packed.at[pl.ds(pl.multiple_of(owner * size, ALIGN), size), :]
        ends = (where, part) if outward else (part, where)
        copies.append(pltpu.make_async_copy(*ends, sems.at[shift]))
    return copies


def compact_kernel(me_ref, quality_ref, v_ref, pos_ref, offs_ref, *rest):
    outs, (tiles, packed, sems, in_sems, offs, offs_sem) = rest[:-6], rest[-6:]
    nblk, block_rows = pos_ref.shape
    rounds = nblk // GROUP
    for copy in group_copies(v_ref, tiles, in_sems):
        copy.start()
    copy = pltpu.make_async_copy(offs_ref, offs, offs_sem)
    plan(quality_ref[...], pos_ref, offs_ref, copy.start)
    packed[:ALIGN, :] = jnp.zeros((ALIGN, packed.shape[1]), packed.dtype)
    copy.wait()

    def body(step, carry):
        group_wait(v_ref, tiles, in_sems, step)
        pos = pos_ref[pl.ds(pl.multiple_of(step * GROUP, GROUP), GROUP), :]
        span = PAIR * block_rows
        made = []
        for i in range(GROUP // PAIR):
            at = pl.multiple_of(step * (GROUP * block_rows) + i * span, span)
            made.append(tiles[pl.ds(at, span), :])
        pack_round(step, rounds, pos, offs, made, packed, outs, sems, me_ref[0])
        return carry

    lax.fori_loop(0, rounds, body, 0)
    for copy in part_copies(packed, outs, sems, me_ref[0], True):
        copy.wait()


def part_shapes(size, count, width):
    return (jax.ShapeDtypeStruct((size, width), jnp.bfloat16),) * count


def compact(v, quality, me, size, count):
    rows, width = v.shape
    nblk, block_rows = quality.shape
    shapes = part_shapes(size, count, width)
    plan_shapes = (
        jax.ShapeDtypeStruct((nblk, block_rows), jnp.int32),
        jax.ShapeDtypeStruct((8, nblk), jnp.int32),
    )
    pos, offs, *parts = pl.pallas_call(
        compact_kernel,
        out_shape=plan_shapes + shapes,
        grid_spec=pltpu.PrefetchScalarGridSpec(
            num_scalar_prefetch=1,
            grid=(1,),
            in_specs=[
                pl.BlockSpec((nblk, block_rows), lambda i, *_: (0, 0)),
                pl.BlockSpec(memory_space=pl.ANY),
            ],
            out_specs=[
                pl.BlockSpec((nblk, block_rows), lambda i, *_: (0, 0)),
                pl.BlockSpec((8, nblk), lambda i, *_: (0, 0)),
            ]
            + [pl.BlockSpec(memory_space=pl.ANY)] * len(shapes),
            scratch_shapes=[
                pltpu.VMEM((rows, width), jnp.bfloat16),
                pltpu.VMEM((rows + ALIGN, width), jnp.bfloat16),
                pltpu.SemaphoreType.DMA((len(shapes),)),
                pltpu.SemaphoreType.DMA((nblk // GROUP,)),
                pltpu.SMEM((8, nblk), jnp.int32),
                pltpu.SemaphoreType.DMA,
            ],
        ),
        compiler_params=params(16),
        cost_estimate=pl.CostEstimate(
            flops=2 * rows * 272 * width, bytes_accessed=4 * rows * width, transcendentals=0
        ),
    )(me, quality, v)
    return pos, offs, tuple(parts)


def load_owner(packed, ins, sems, me, owner):
    count = len(ins)
    size = ins[0].shape[0]
    for shift, part in enumerate(ins):

        @pl.when(lax.rem(me + count - shift, count) == owner)
        def _():
            pltpu.make_async_copy(
                part, packed.at[pl.ds(owner * size, size), :], sems.at[owner]
            ).start()


def expand_kernel(me_ref, offs_ref, pos_ref, *rest):
    ins, (out_ref, packed, tiles, sems, out_sems) = rest[:-5], rest[-5:]
    nblk, block_rows = pos_ref.shape
    rounds = nblk // GROUP
    span = EXPAND * block_rows
    held = len(ins) * ins[0].shape[0]
    size = ins[0].shape[0]
    for piece in range(len(ins)):
        load_owner(packed, ins, sems, me_ref[0], piece)
    clear(packed, held)

    def need(step):
        end = window(offs_ref, (step + 1) * GROUP - EXPAND) + span + ALIGN
        return jnp.where(step == rounds - 1, held, jnp.minimum(end, held))

    def arrive(step):
        before = jnp.where(step == 0, 0, need(jnp.maximum(step - 1, 0)))
        now = need(step)
        for owner in range(len(ins)):

            @pl.when((owner * size >= before) & (owner * size < now))
            def _():
                pltpu.make_async_copy(
                    ins[0], packed.at[pl.ds(owner * size, size), :], sems.at[owner]
                ).wait()

    def body(step, carry):
        arrive(step)
        pos = pos_ref[pl.ds(pl.multiple_of(step * GROUP, GROUP), GROUP), :]
        made = []
        for i in range(0, GROUP, EXPAND):
            start = window(offs_ref, step * GROUP + i)
            row = jnp.concatenate([pos[i + j : i + j + 1, :] for j in range(EXPAND)], axis=1)
            at = lax.broadcasted_iota(jnp.int32, (span + ALIGN, span), 0) + start
            chosen = jnp.where(at == row, 1.0, 0.0).astype(jnp.bfloat16)
            made.append(
                lax.dot_general(
                    chosen,
                    packed[pl.ds(start, span + ALIGN), :],
                    (((0,), (0,)), ((), ())),
                    preferred_element_type=jnp.float32,
                ).astype(jnp.bfloat16)
            )
        step_rows = GROUP * block_rows
        base = pl.multiple_of(step * step_rows, step_rows)
        for i, rows in enumerate(made):
            tiles[pl.ds(pl.multiple_of(base + i * span, span), span), :] = rows
        pltpu.make_async_copy(
            tiles.at[pl.ds(base, step_rows)],
            out_ref.at[pl.ds(base, step_rows)],
            out_sems.at[step],
        ).start()
        return carry

    lax.fori_loop(0, rounds, body, 0)
    for copy in group_copies(tiles, out_ref, out_sems):
        copy.wait()


def expand(parts, pos, offs, me):
    nblk, block_rows = pos.shape
    rows = nblk * block_rows
    width = parts[0].shape[1]
    return pl.pallas_call(
        expand_kernel,
        out_shape=jax.ShapeDtypeStruct((rows, width), jnp.bfloat16),
        grid_spec=pltpu.PrefetchScalarGridSpec(
            num_scalar_prefetch=2,
            grid=(1,),
            in_specs=[pl.BlockSpec((nblk, block_rows), lambda i, *_: (0, 0))]
            + [pl.BlockSpec(memory_space=pl.ANY)] * len(parts),
            out_specs=pl.BlockSpec(memory_space=pl.ANY),
            scratch_shapes=[
                pltpu.VMEM((rows + ALIGN, width), jnp.bfloat16),
                pltpu.VMEM((rows, width), jnp.bfloat16),
                pltpu.SemaphoreType.DMA((len(parts),)),
                pltpu.SemaphoreType.DMA((nblk // GROUP,)),
            ],
        ),
        compiler_params=params(16),
        cost_estimate=pl.CostEstimate(
            flops=2 * rows * 256 * width, bytes_accessed=4 * rows * width, transcendentals=0
        ),
    )(me, offs, pos, *parts)


def rounds_of(nblk, compacting):
    return nblk // GROUP if compacting else max(nblk // (2 * GROUP), 1)


def spatial_kernel(
    compacting, me_ref, offs_ref, ids_ref, counts_ref, pos_ref, weight_ref, near, own, far, _, *rest
):
    nblk, block_rows = pos_ref.shape
    slots = weight_ref.shape[1]
    rounds = rounds_of(nblk, compacting)
    group = nblk // rounds
    scratch = 6
    outs, (tiles, weights, halo_sems, weight_sems, made, sems) = rest[:-scratch], rest[-scratch:]
    rows = tiles.shape[0] // 3
    loads = group_copies(weight_ref, weights, weight_sems)
    loads[0].start()
    halo = [
        pltpu.make_async_copy(source, tiles.at[pl.ds(i * rows, rows), :], halo_sems.at[i])
        for i, source in enumerate((near, own, far))
    ]
    for copy in halo + loads[1:]:
        copy.start()
    if compacting:
        made[:ALIGN, :] = jnp.zeros((ALIGN, made.shape[1]), made.dtype)
    for copy in halo:
        copy.wait()

    def product(step, i):
        block = step * group + i
        used = counts_ref[block]
        live = []
        picked = []
        for slot in range(slots):
            at = ids_ref[block * slots + slot]
            scale = jnp.where(slot < used, 1.0, 0.0).astype(jnp.bfloat16)
            live.append(weights[block, slot] * scale)
            start = pl.multiple_of(at * block_rows, block_rows)
            picked.append(tiles[pl.ds(start, block_rows), :])
        return jnp.dot(
            jnp.concatenate(live, axis=1),
            jnp.concatenate(picked, axis=0),
            preferred_element_type=jnp.float32,
        ).astype(jnp.bfloat16)

    def body(step, carry):
        group_wait(weight_ref, weights, weight_sems, step)
        pos = pos_ref[pl.ds(pl.multiple_of(step * group, group), group), :]
        found = [product(step, i) for i in range(group)]
        if compacting:
            found = [
                jnp.concatenate(found[i : i + PAIR], axis=0) for i in range(0, group, PAIR)
            ]
            pack_round(step, rounds, pos, offs_ref, found, made, outs, sems, me_ref[0])
            return carry
        size = group * block_rows
        base = pl.multiple_of(step * size, size)
        for i in range(group):
            kept = jnp.where(pos[i : i + 1, :] >= 0, 1.0, 0.0)
            kept = jnp.broadcast_to(kept, (block_rows, block_rows)).T.astype(jnp.bfloat16)
            kept = jnp.concatenate([kept] * (made.shape[1] // block_rows), axis=1)
            made[pl.ds(pl.multiple_of(base + i * block_rows, block_rows), block_rows), :] = (
                found[i] * kept
            )
        pltpu.make_async_copy(
            made.at[pl.ds(base, size)], outs[0].at[pl.ds(base, size)], sems.at[step]
        ).start()
        return carry

    lax.fori_loop(0, rounds, body, 0)
    if compacting:
        copies = part_copies(made, outs, sems, me_ref[0], True)
    else:
        copies = group_copies(made, outs[0], sems)
    for copy in copies:
        copy.wait()


def spatial(halo, weights, ids, counts, pos, offs, me, size, count):
    rows, width = halo[1].shape
    nblk, block_rows = pos.shape
    slots = weights.shape[1]
    any_spec = pl.BlockSpec(memory_space=pl.ANY)
    rounds = rounds_of(nblk, size is not None)
    if size is None:
        shapes = (jax.ShapeDtypeStruct((rows, width), jnp.bfloat16),)
        made = (rows, rounds)
    else:
        shapes = part_shapes(size, count, width)
        made = (rows + ALIGN, len(shapes))
    return pl.pallas_call(
        functools.partial(spatial_kernel, size is not None),
        out_shape=shapes,
        grid_spec=pltpu.PrefetchScalarGridSpec(
            num_scalar_prefetch=4,
            grid=(1,),
            in_specs=[pl.BlockSpec((nblk, block_rows), lambda i, *_: (0, 0))] + [any_spec] * 5,
            out_specs=[any_spec] * len(shapes),
            scratch_shapes=[
                pltpu.VMEM((3 * rows, width), jnp.bfloat16),
                pltpu.VMEM(weights.shape, jnp.bfloat16),
                pltpu.SemaphoreType.DMA((3,)),
                pltpu.SemaphoreType.DMA((rounds,)),
                pltpu.VMEM((made[0], width), jnp.bfloat16),
                pltpu.SemaphoreType.DMA((made[1],)),
            ],
        ),
        compiler_params=params(34),
        cost_estimate=pl.CostEstimate(
            flops=2 * rows * slots * block_rows * width,
            bytes_accessed=8 * rows * width + 2 * rows * slots * block_rows,
            transcendentals=0,
        ),
    )(me, offs, ids, counts, pos, weights, *halo)


def mix_kernel(count, me_ref, op_ref, *rest):
    ins, outs, (rolled, sems) = rest[:count], rest[count : 2 * count], rest[2 * count :]
    width = ins[0].shape[1]
    me = me_ref[0]

    @pl.when(pl.program_id(0) == 0)
    def _():
        copies = []
        for shift in range(count):
            source = lax.rem(me + count - shift, count)
            copies.append(
                pltpu.make_async_copy(
                    op_ref.at[pl.ds(pl.multiple_of(source * width, ALIGN), width), :],
                    rolled.at[pl.ds(shift * width, width), :],
                    sems.at[shift],
                )
            )
        for copy in copies:
            copy.start()
        for copy in copies:
            copy.wait()

    row = jnp.concatenate([part[...] for part in ins], axis=1)
    for shift in range(count):
        dest = lax.rem(me + shift, count)
        columns = rolled[:, pl.ds(pl.multiple_of(dest * width, 128), width)]
        outs[shift][...] = jnp.dot(row, columns, preferred_element_type=jnp.float32).astype(
            jnp.bfloat16
        )


def mix(parts, chan_op, me):
    count = len(parts)
    rows, width = parts[0].shape
    tiles = [t for t in range(ALIGN, min(rows, 640) + 1, ALIGN) if rows % t == 0]
    tile = tiles[-1]
    spec = pl.BlockSpec((tile, width), lambda i, *_: (i, 0))
    return pl.pallas_call(
        functools.partial(mix_kernel, count),
        out_shape=part_shapes(rows, count, width),
        grid_spec=pltpu.PrefetchScalarGridSpec(
            num_scalar_prefetch=1,
            grid=(rows // tile,),
            in_specs=[pl.BlockSpec(memory_space=pl.ANY)] + [spec] * count,
            out_specs=[spec] * count,
            scratch_shapes=[
                pltpu.VMEM(chan_op.shape, jnp.bfloat16),
                pltpu.SemaphoreType.DMA((count,)),
            ],
        ),
        compiler_params=params(16),
        cost_estimate=pl.CostEstimate(flops=1, bytes_accessed=1, transcendentals=0),
    )(me, chan_op, *parts)


class Line:
    def __init__(self, depth):
        self.depth = depth
        self.done = []

    def exchange(self, parts):
        count = len(parts)
        arrived = list(parts)
        for shift in sorted(range(1, count), key=lambda k: min(k, count - k)):
            part = parts[shift]
            if len(self.done) >= self.depth:
                part = after(part, self.done[-self.depth])
            arrived[shift] = lax.ppermute(
                part, "chan", [(i, (i + shift) % count) for i in range(count)]
            )
            self.done.append(arrived[shift])
        return tuple(arrived)


def after(values, *others):
    return lax.optimization_barrier((values, others))[0]


def gate_kernel(x_ref, out_ref):
    out_ref[...] = x_ref[...]


def gate(x):
    shape = (ALIGN, x.shape[1])
    spec = pl.BlockSpec(shape, lambda i: (0, 0))
    return pl.pallas_call(
        gate_kernel,
        out_shape=jax.ShapeDtypeStruct(shape, x.dtype),
        grid=(1,),
        in_specs=[spec],
        out_specs=spec,
        cost_estimate=pl.CostEstimate(flops=10**11, bytes_accessed=1, transcendentals=0),
    )(x)


def halo_of(x):
    count = lax.axis_size("orbit")
    far = [(i, i + 1) for i in range(1, count - 1, 2)]
    far = lax.ppermute(x, "orbit", far + [(b, a) for a, b in far])
    near = [(i, i + 1) for i in range(0, count - 1, 2)]
    near = lax.ppermute(x, "orbit", near + [(b, a) for a, b in near])
    return near, x, far


def halo_ids(neighbours, nblk):
    mine = lax.axis_index("orbit")
    local = jnp.clip(neighbours - (mine - 1) * nblk, 0, 3 * nblk - 1)
    side = local // nblk
    side = jnp.where(mine % 2 == 0, 2 - side, side)
    return (side * nblk + local % nblk).reshape(-1)


def weigh(
    innovation, perturbation, quality, neighbours, counts, spatial_blocks, chan_op, capacity, watch
):
    rows, width = innovation.shape
    block_rows = spatial_blocks.shape[2]
    nblk = rows // block_rows
    count = lax.axis_size("chan")
    size = capacity // count

    me = lax.axis_index("chan").astype(jnp.int32).reshape(1)
    ids = halo_ids(neighbours, nblk)

    def spread(halo, room):
        return spatial(halo, spatial_blocks, ids, counts, pos, offs, me, room, count)

    kept = quality.reshape(nblk, block_rows)
    pos, offs, parts_i = compact(innovation, kept, me, size, count)
    line = Line(DEPTH)
    there_i = line.exchange(parts_i)
    perturbation, quality = after((perturbation, quality), parts_i[0])
    masked_p = perturbation * quality.astype(jnp.bfloat16)[:, None]
    parts_p = spread((*halo_of(masked_p), gate(there_i[1 % count])), size)
    there_p = line.exchange(parts_p)

    mixed_i = mix(after(there_i, parts_p[0]), chan_op, me)
    back_i = line.exchange(mixed_i)
    seen = watch(after(quality, parts_p[0]))
    mixed_p = mix(after(there_p, (mixed_i[0], seen)), chan_op, me)
    back_p = line.exchange(after(mixed_p, back_i))

    wide_i = expand(after(back_i, mixed_p[0]), pos, offs, me)
    (out_i,) = spread((*halo_of(wide_i), gate(back_p[count // 2])), None)
    out_p = expand(after(back_p, out_i), pos, offs, me)
    return (out_i, out_p), seen


def shards(innovation, perturbation, quality, *others):
    rows = innovation.shape[0]
    unit = ALIGN * lax.axis_size("chan")
    capacity = -(-rows * 57 // (64 * unit)) * unit
    given = (innovation, perturbation, quality, *others)

    def overfull(quality):
        more = jnp.sum(quality, dtype=jnp.int32) > capacity
        return lax.pmax(more.astype(jnp.int32), ("grp", "orbit"))

    packed, more = weigh(*given, capacity, overfull)
    return lax.cond(
        more > 0,
        lambda given, packed: weigh(*given, rows, lambda quality: None)[0],
        lambda given, packed: packed,
        given,
        packed,
    )


def solution(mesh):
    placed = (
        P(("grp", "orbit"), "chan"),
        P(("grp", "orbit"), "chan"),
        P(("grp", "orbit")),
        P(("grp", "orbit"), None),
        P(("grp", "orbit")),
        P(("grp", "orbit"), None, None, None),
        P(),
    )
    return jax.shard_map(
        shards,
        mesh=mesh,
        in_specs=placed,
        out_specs=(P(("grp", "orbit"), "chan"), P(("grp", "orbit"), "chan")),
        check_vma=False,
    )
```
